512 devices in a mesh: dp: 64 (over y_hi, z, core), tensor: 8 (over x, y_lo).
Axes of the slice: x: 4, y: 4 (y_hi: 2, y_lo: 2; y = y_hi * 2 + y_lo), z: 16, core: 2. Of those that a mesh axis runs over, the one named last changes fastest.
Arguments:
- hidden: bfloat16 [16384, 8192], P('dp', 'tensor'), may hold values from -600 to 600, as said below
- norm_gain: bfloat16 [8192], replicated, may hold values from 0.099609375 to 1.8984375
- query_weight: bfloat16 [8192, 4096], P(('dp', 'tensor')), may hold values from -0.0625 to 0.0625
- key_weight: bfloat16 [8192, 1024], P(('dp', 'tensor')), may hold values from -0.0625 to 0.0625
- value_weight: bfloat16 [8192, 1024], P(('dp', 'tensor')), may hold values from -0.0625 to 0.0625
- query_bias: bfloat16 [4096], P('tensor'), may hold values from -2 to 8, as said below
- key_bias: bfloat16 [1024], P('tensor'), may hold values from -2 to 6, as said below
- value_bias: bfloat16 [1024], P('tensor'), may hold values from -3 to 3
- lengths: int32 [64, 4], P('dp'), may hold values from 1 to 128, 256 in all within a row
- page_table: int32 [64, 16], P('dp'), may hold values from 0 to 15, each once within a row
Outputs:
- attention: bfloat16 [16384, 4096], P('dp', 'tensor')
- cache_pages: bfloat16 [1024, 32, 2048], P('dp', None, 'tensor')
The draws below stay inside these ranges and needn't reach their ends.
Inputs may be any that keep to these rules, and one draw needn't show every extreme that they name: `hidden`: the custom draw of the layer input. `query_bias`: the custom draw of the query bias. `key_bias`: the custom draw of the key bias. Each replica's lengths sum to 256, and its longest rollout has exactly 128 tokens. `page_table`: each replica's row is a permutation of its 16 pages.
All inputs are finite; a program needn't handle non-finite values.
Results may differ from the reference program's by a relative error of at most 0.0088.
Values may be sent and summed in bfloat16 or wider, within the bound.
A program may use at most 64 MiB of HBM per device.

```python
import math
import jax
import jax.numpy as jnp
import numpy as np
from jax import lax

D = 8192
KVH = 8
HD = 128
QH = 32
ROLLS = 4
PAGE = 32
TOK_REP = 256
LMAX = 128
BLOCKS = 4
PAGES_REP = 16
REPLICAS = 64
TOKENS = 16384
PAGES = 1024
N_DP = 64


def draw_hidden(key, part):
    key_base, key_rows, key_cols = jax.random.split(key, 3)
    base = jnp.clip(jax.random.normal(key_base, (TOKENS, D), jnp.float32), -6.0, 6.0)
    row_scale = jnp.exp(jax.random.uniform(key_rows, (TOKENS, 1), jnp.float32) * math.log(10.0))
    col_scale = jnp.exp(jax.random.uniform(key_cols, (1, D), jnp.float32) * math.log(10.0))
    return (base * row_scale * col_scale).astype(jnp.bfloat16)


def draw_query_bias(key, part):
    key_noise = jax.random.fold_in(jax.random.fold_in(key, 11), 0)
    noise = 0.5 * jnp.clip(jax.random.normal(key_noise, (QH * HD,), jnp.float32), -4.0, 4.0)
    return noise.astype(jnp.bfloat16)


def draw_key_bias(key, part):
    key_noise = jax.random.fold_in(key, 23)
    noise = 0.5 * jnp.clip(jax.random.normal(key_noise, (KVH * HD,), jnp.float32), -4.0, 4.0)
    return noise.astype(jnp.bfloat16)


def block_levels(rng, shape, pieces, smallest, top_value):
    def one(axis_at, blocks):
        heights = jax.random.uniform(jax.random.fold_in(jax.random.fold_in(rng, 6), axis_at), (blocks,), jnp.float32, smallest / len(pieces), top_value / len(pieces))
        return jnp.repeat(jnp.exp(heights), shape[axis_at] // blocks).reshape((-1,) + (1,) * (len(shape) - axis_at - 1))

    level = one(*pieces[0])
    for cut in pieces[1:]:
        level = level * one(*cut)
    return level


def length_profile(amount, total, reach, lean):
    weights = [(1 << 20) // math.isqrt(rank ** lean) + 1 for rank in range(2, amount + 1)]
    surplus, counts = total - reach - (amount - 1), [1] * (amount - 1)
    while surplus > 0:
        free = [i for i in range(amount - 1) if counts[i] < reach]
        mass, budget = sum([weights[i] for i in free]), surplus
        for i in free:
            more = min(reach - counts[i], max(1, budget * weights[i] // mass), surplus)
            counts[i] = counts[i] + more
            surplus = surplus - more
    return np.array([reach] + counts)


def uneven(own_key, count, total, bound, slope):
    if count == 2:
        one = jax.random.randint(own_key, (), max(1, total - bound), min(bound, total - 1) + 1)
        return jnp.stack([one, total - one])
    sizes = jnp.asarray(length_profile(count, total, bound, slope), jnp.int32)
    pairs = (count - 1) // 2
    donor, receiver = sizes[1:1 + 2 * pairs:2], sizes[2:2 + 2 * pairs:2]
    room = jnp.minimum(donor - 1, bound - receiver)
    passed = jax.random.randint(jax.random.fold_in(own_key, 1), (pairs,), 0, 1 << 20) % (room + 1)
    sizes = sizes.at[1:1 + 2 * pairs:2].set(donor - passed).at[2:2 + 2 * pairs:2].set(receiver + passed)
    return sizes[jax.random.permutation(jax.random.fold_in(own_key, 2), count)]


def bell_draw(key, shape, deviation, bound, shards=(), held_as=jnp.bfloat16):
    values = deviation * jax.random.normal(key, shape, jnp.float32)
    if shards:
        values = values * block_levels(key, shape, shards, -0.22, 0.18)
    return jnp.clip(values, -bound, bound).astype(held_as)


def setup_inputs(seed: int = 0) -> dict:
    splits = jax.random.split(jax.random.key(seed), 11)
    hidden = draw_hidden(jax.random.fold_in(splits[10], 71), 0)
    norm_gain = jnp.clip(1.0 + 0.18 * jax.random.normal(splits[1], (D,), jnp.float32), 0.099609375, 1.8984375).astype(jnp.bfloat16)
    query_weight = bell_draw(splits[2], (D, QH * HD), D ** -0.5, 0.0625, ((0, 512),))
    key_weight = bell_draw(splits[3], (D, KVH * HD), D ** -0.5, 0.0625, ((0, 512),))
    value_weight = bell_draw(splits[4], (D, KVH * HD), D ** -0.5, 0.0625, ((0, 512),))
    query_bias = draw_query_bias(jax.random.fold_in(splits[10], 71), 0)
    key_bias = draw_key_bias(jax.random.fold_in(splits[10], 71), 0)
    value_bias = bell_draw(splits[7], (KVH * HD,), 0.5, 3.0, ((0, 8),))
    lengths = jax.vmap(lambda own: uneven(own, ROLLS, TOK_REP, LMAX, 2))(jax.random.split(splits[8], REPLICAS)).reshape((REPLICAS, ROLLS)).astype(jnp.int32)
    page_table = jax.vmap(lambda own: jax.random.permutation(own, PAGES_REP))(jax.random.split(splits[9], REPLICAS)).reshape((REPLICAS, PAGES_REP)).astype(jnp.int32)
    return {"hidden": hidden, "norm_gain": norm_gain, "query_weight": query_weight, "key_weight": key_weight, "value_weight": value_weight, "query_bias": query_bias, "key_bias": key_bias, "value_bias": value_bias, "lengths": lengths, "page_table": page_table}


rope_base = 1000000.0

def rotary(values_f, positions):
    halfway = HD // 2
    frequency = rope_base ** (-(jnp.arange(halfway, dtype=jnp.float32) * 2.0 / HD))
    angles = positions.astype(jnp.float32)[:, None] * frequency[None, :]
    cosine = jnp.cos(angles)[:, None, :]
    sine_part = jnp.sin(angles)[:, None, :]
    lower_half = values_f[..., :halfway]
    upper_half = values_f[..., halfway:]
    return jnp.concatenate([lower_half * cosine - upper_half * sine_part, upper_half * cosine + lower_half * sine_part], axis=-1)

def segments_of(length_row, token_count):
    ends = jnp.cumsum(length_row).astype(jnp.int32)
    starts = (ends - length_row).astype(jnp.int32)
    tok_index = jnp.arange(token_count, dtype=jnp.int32)
    segment = lax.optimization_barrier(jnp.sum((tok_index[None, :] >= ends[:, None]).astype(jnp.int32), axis=0))
    onehot = segment[:, None] == jnp.arange(ROLLS, dtype=jnp.int32)[None, :]
    leading = lax.optimization_barrier(jnp.sum(jnp.where(onehot, starts[None, :], 0), axis=1)).astype(jnp.int32)
    return (segment, tok_index - leading, starts)

def attention_of(queries, key_rows, value_rows, segment):
    token_count = queries.shape[0]
    kv_heads = key_rows.shape[1]
    group_size = queries.shape[1] // kv_heads
    grouped = queries.reshape(token_count, kv_heads, group_size, HD).astype(jnp.float32)
    scores = jnp.einsum('ikgd,jkd->kgij', grouped, key_rows.astype(jnp.float32)) * HD ** (-0.5)
    tok_index = jnp.arange(token_count, dtype=jnp.int32)
    allowed = (segment[:, None] == segment[None, :]) & (tok_index[None, :] <= tok_index[:, None])
    scores = jnp.where(allowed[None, None], scores, -1e+30)
    row_max = lax.optimization_barrier(jnp.max(scores, axis=-1, keepdims=True))
    weights = jnp.exp(scores - row_max)
    weights = (weights / lax.optimization_barrier(jnp.sum(weights, axis=-1, keepdims=True))).astype(jnp.bfloat16)
    mixed = jnp.einsum('kgij,jkd->ikgd', weights.astype(jnp.float32), value_rows.astype(jnp.float32))
    return mixed.reshape(token_count, kv_heads * group_size * HD).astype(jnp.bfloat16)

def pages_of(kv_rows, length_row, starts, page_row):
    slots = jnp.arange(PAGES_REP, dtype=jnp.int32)
    owner = slots // BLOCKS
    within = slots % BLOCKS
    offsets = within[:, None] * PAGE + jnp.arange(PAGE, dtype=jnp.int32)[None, :]
    onehot = owner[:, None] == jnp.arange(ROLLS, dtype=jnp.int32)[None, :]
    owner_len = lax.optimization_barrier(jnp.sum(jnp.where(onehot, length_row[None, :], 0), axis=1)).astype(jnp.int32)
    owner_start = lax.optimization_barrier(jnp.sum(jnp.where(onehot, starts[None, :], 0), axis=1)).astype(jnp.int32)
    valid_slot = offsets < owner_len[:, None]
    source = jnp.where(valid_slot, owner_start[:, None] + offsets, 0).astype(jnp.int32)
    blocks_out = jnp.where(valid_slot[..., None], kv_rows[source], jnp.zeros((), jnp.bfloat16))
    empty = jnp.zeros((PAGES_REP, PAGE, kv_rows.shape[1]), jnp.bfloat16)
    return empty.at[page_row].set(blocks_out)

def reference(hidden, norm_gain, query_weight, key_weight, value_weight, query_bias, key_bias, value_bias, lengths, page_table):

    def replica(inputs):
        tokens, length_row, page_row = inputs
        tokens_f = tokens.astype(jnp.float32)
        meansq = lax.optimization_barrier(jnp.mean(tokens_f * tokens_f, axis=-1, keepdims=True))
        normed = (tokens_f * lax.rsqrt(meansq + 1e-06) * norm_gain.astype(jnp.float32)).astype(jnp.bfloat16)
        segment, position, starts = segments_of(length_row, TOK_REP)
        queries = jnp.dot(normed, query_weight, preferred_element_type=jnp.float32) + query_bias.astype(jnp.float32)
        queries = rotary(queries.reshape(TOK_REP, QH, HD), position).astype(jnp.bfloat16)
        key_rows = jnp.dot(normed, key_weight, preferred_element_type=jnp.float32) + key_bias.astype(jnp.float32)
        key_rows = rotary(key_rows.reshape(TOK_REP, KVH, HD), position).astype(jnp.bfloat16)
        value_rows = (jnp.dot(normed, value_weight, preferred_element_type=jnp.float32) + value_bias.astype(jnp.float32)).astype(jnp.bfloat16)
        value_rows = value_rows.reshape(TOK_REP, KVH, HD)
        mixed = attention_of(queries, key_rows, value_rows, segment)
        kv_rows = jnp.stack([key_rows, value_rows], axis=2).reshape(TOK_REP, KVH * 2 * HD)
        return (mixed, pages_of(kv_rows, length_row, starts, page_row))
    mixed_all, pages_all = lax.map(replica, (hidden.reshape(N_DP, TOK_REP, D), lengths, page_table))
    return (mixed_all.reshape(TOKENS, QH * HD), pages_all.reshape(PAGES, PAGE, KVH * 2 * HD))
```

```python
import functools
import math

import jax
import jax.numpy as jnp
from jax import lax
from jax.experimental import pallas as pl
from jax.experimental.pallas import tpu as pltpu
from jax.sharding import PartitionSpec as P

MESH = pl.DeviceIdType.MESH
HD = 128
ROLLS = 4
PAGE = 32
BLOCKS = 4
PAGES_REP = 16
TOK = 256
D = 8192
NZ = 16
BASE = 1000000.0
F32 = jnp.float32
BF16 = jnp.bfloat16
NEG = -1e30


def rem(a, n):
    return lax.rem(a, n)


def kernel(
    h_ref, gain_ref, wq_ref, wk_ref, wv_ref, bq_ref, bk_ref, bv_ref, len_ref, pt_ref,
    att_ref, page_ref,
    ws, wb, hs, a5, a2, ps, rs, ssb, cos_t, sin_t, mask_t, hot_t, kv_t,
    ws_send, ws_send_self, ws_recv, z_send, z_recv, c_send, c_recv, h_send, h_recv, p_send, p_recv, s_send, s_recv,
):
    dp = lax.axis_index("dp")
    t = lax.axis_index("tensor")
    y_hi, z, core = dp // (2 * NZ), rem(dp // 2, NZ), rem(dp, 2)
    x, y_lo = t // 2, rem(t, 2)

    def dev(x, y_lo, y_hi, z, core):
        return ((y_hi * NZ + z) * 2 + core, x * 2 + y_lo)

    def flip(bit, by):
        return rem(bit + by, 2)

    barrier = pltpu.get_barrier_semaphore()
    peers = []
    for r in range(1, 32):
        peers.append(dev(rem(x + r % 4, 4), flip(y_lo, r // 4 % 2), flip(y_hi, r // 8 % 2), z, flip(core, r // 16)))
    up, down = rem(z + 1, NZ), rem(z + NZ - 1, NZ)
    up_dev, down_dev = dev(x, y_lo, y_hi, up, core), dev(x, y_lo, y_hi, down, core)
    peers += [up_dev, down_dev]
    for d in peers:
        pl.semaphore_signal(barrier, inc=1, device_id=d, device_id_type=MESH)

    g = gain_ref[...].astype(F32)
    g_row = jnp.sum(jnp.where(lax.broadcasted_iota(jnp.int32, g.shape, 0) == dp, g, 0.0), axis=0, keepdims=True)
    lane = lax.broadcasted_iota(jnp.int32, (16, 128), 1)
    sub = lax.broadcasted_iota(jnp.int32, (16, 128), 0)
    g_col = jnp.sum(jnp.where(lane == sub + 16 * t, g_row, 0.0), axis=1, keepdims=True)
    for yh_d in range(2):
        for yl_d in range(2):
            for k in range(2):
                for e in range(2):
                    td = 4 * k + 2 * e + yl_d
                    first = (wk_ref if yh_d == 0 else wv_ref)[:, 128 * td : 128 * td + 128]
                    q0 = 512 * td + 256 * yh_d
                    parts = (first, wq_ref[:, q0 : q0 + 128], wq_ref[:, q0 + 128 : q0 + 256])
                    for j in range(3):
                        ws[(yh_d * 2 + yl_d) * 2 + k, j, :, 128 * e : 128 * e + 128] = (
                            parts[j].astype(F32) * g_col
                        ).astype(BF16)
    for b in range(2):
        for u in range(4):
            hs[b, u] = h_ref[:, 256 * u + 128 * b : 256 * u + 128 * b + 128]

    pl.semaphore_wait(barrier, len(peers))

    def remote(src, dst, send, recv, device):
        pltpu.make_async_remote_copy(
            src_ref=src, dst_ref=dst, send_sem=send, recv_sem=recv, device_id=device, device_id_type=MESH
        ).start()

    def wait(ref, sem):
        pltpu.make_async_copy(ref, ref, sem).wait()

    x_dst = 2 * y_hi + core
    slot_w = pl.ds(pl.multiple_of(16 * t, 16), 16)
    for r in range(8):
        yl_d, yh_d, k = flip(y_lo, r % 2), flip(y_hi, r // 2 % 2), flip(core, r // 4)
        src = ws.at[(yh_d * 2 + yl_d) * 2 + k]
        dst = wb.at[:, k, slot_w, :]
        to = dev(x_dst, yl_d, yh_d, z, k)
        if r > 0:
            remote(src, dst, ws_send, ws_recv, to)
        else:

            @pl.when(x == x_dst)
            def _():
                pltpu.make_async_copy(src, dst, ws_recv).start()

            @pl.when(x != x_dst)
            def _():
                remote(src, dst, ws_send_self, ws_recv, to)

    xb = rem(x, 2)
    x_pair = x + 1 - 2 * xb
    piece = 4 * (y_hi * 4 + rem(t, 4))
    for r in (1, 2, 3, 4, 5, 6, 7):
        xd = x if r < 4 else x_pair
        src = hs.at[xb if r < 4 else 1 - xb]
        to = dev(xd, flip(y_lo, r % 2), flip(y_hi, r // 2 % 2), z, core)
        remote(src, a5.at[pl.ds(piece, 4)], h_send, h_recv, to)
    for u in range(4):
        a5[piece + u] = hs[xb, u]

    me = core
    other = 1 - core

    def rows(p, half, lo=0, n=128):
        return pl.ds(p * 256 + half * 128 + lo, n)

    def z_copy(way, j, src_rows, dst_rows, sub_id, step):
        remote(
            wb.at[j, me, src_rows, :], wb.at[j, me, dst_rows, :], z_send, z_recv.at[way, sub_id, step - 1],
            up_dev if way == 0 else down_dev,
        )

    def to_core(j, at):
        remote(wb.at[j, me, at, :], wb.at[j, me, at, :], c_send, c_recv.at[j], dev(x, y_lo, y_hi, z, other))

    wait(wb.at[:, me, rows(0, 0), :], ws_recv)
    for j in range(2):
        for way in range(2):
            z_copy(way, j, rows(0, 0), rows(1, way), j, 1)

    h = h_ref[...].astype(F32)
    sq = h * h
    hi = sq.astype(BF16)
    lo = (sq - hi.astype(F32)).astype(BF16)
    ones = jnp.ones((8, 1024), BF16)
    nt = (((1,), (1,)), ((), ()))
    ssb[0] = lax.dot_general(ones, hi, nt, preferred_element_type=F32) + lax.dot_general(
        ones, lo, nt, preferred_element_type=F32
    )
    for r in range(1, 8):
        remote(ssb.at[0], ssb.at[r], s_send, s_recv, dev(rem(x + r % 4, 4), flip(y_lo, r // 4), y_hi, z, core))
    for j in range(3):
        to_core(j, rows(0, 0))

    def first_tables():
        ends, starts, total = [], [], 0
        for r in range(ROLLS):
            starts.append(total)
            total = total + len_ref[0, r]
            ends.append(total)
        tok = lax.broadcasted_iota(jnp.int32, (TOK, 128), 0)
        begin = jnp.zeros((TOK, 128), jnp.int32)
        for r in range(1, ROLLS):
            begin = jnp.where(tok >= ends[r - 1], starts[r], begin)
        d = lax.broadcasted_iota(jnp.int32, (TOK, 128), 1)
        half = rem(d, 64).astype(F32)
        freq = jnp.exp(half * (-2.0 / HD * math.log(BASE)))
        angle = (tok - begin).astype(F32) * freq
        cos_t[...] = jnp.cos(angle)
        s = jnp.sin(angle)
        sin_t[...] = jnp.where(d < 64, -s, s)
        for q in range(2):
            col = d + 128 * q
            mask_t[:, 128 * q : 128 * q + 128] = jnp.where((col >= begin) & (col <= tok), 0.0, NEG)

    def page_tables():
        ends, starts, total = [], [], 0
        for r in range(ROLLS):
            starts.append(total)
            total = total + len_ref[0, r]
        n = lax.broadcasted_iota(jnp.int32, (PAGES_REP * PAGE, 128), 0)
        page, slot = n // PAGE, rem(n, PAGE)
        src = jnp.full(n.shape, -1, jnp.int32)
        for e in range(PAGES_REP):
            r, b = e // BLOCKS, e % BLOCKS
            at = b * PAGE + slot
            src = jnp.where((page == pt_ref[0, e]) & (at < len_ref[0, r]), starts[r] + at, src)
        col = lax.broadcasted_iota(jnp.int32, (PAGES_REP * PAGE, 128), 1)
        for q in range(2):
            hot_t[:, 128 * q : 128 * q + 128] = jnp.where(src == col + 128 * q, 1.0, 0.0).astype(BF16)

    def wait_hidden():
        wait(a5.at[pl.ds(0, 28)], h_recv)

    def relay(tk):
        for p in range(8):
            m1 = rem(z + NZ - p, NZ)
            m2 = rem(z + p, NZ) if p else rem(z + 8, NZ)
            a2[tk, :, 256 * p : 256 * p + 128] = a5[tk * NZ + m1]
            a2[tk, :, 256 * p + 128 : 256 * p + 256] = a5[tk * NZ + m2]

    def product(j, k):
        if k == 0:
            wait(wb.at[j, other], c_recv.at[j])

        @pl.loop(0, 2)
        def _(tk):
            part = jnp.dot(a2[tk], wb[j, k], preferred_element_type=F32).astype(BF16)
            for e in range(2):
                ps[j, tk * 4 + 2 * k + e] = part[:, 128 * e : 128 * e + 128]

    def send_parts(j):
        for r in range(7, 0, -1):
            xd, yh_d = rem(x + r % 4, 4), flip(y_hi, r // 4)
            remote(ps.at[j, yh_d * 4 + xd], rs.at[j, r], p_send, p_recv.at[j], dev(xd, y_lo, yh_d, z, core))

    def both(tasks):
        def run():
            for f in tasks:
                f()

        return run

    P_ = functools.partial
    groups = (
        ([(0, 0, 128), (1, 0, 128)], {1: first_tables, 3: page_tables}),
        (
            [(2, 0, 64), (2, 64, 64)],
            {
                1: both([wait_hidden, P_(relay, 0)]),
                2: both([P_(relay, 1), P_(product, 0, 0)]),
                3: both([P_(product, 0, 1), P_(send_parts, 0)]),
                4: P_(product, 1, 0),
                5: both([P_(product, 1, 1), P_(send_parts, 1)]),
            },
        ),
    )
    for gi, (subs, tasks) in enumerate(groups):
        for step in range(1, 9):
            for si, (j, lo_row, n) in enumerate(subs):
                for way in range(2):
                    sem = z_recv.at[way, 2 * gi + si, step - 1]
                    if step < 8:
                        at = rows(step, way, lo_row, n)
                        wait(wb.at[j, me, at, :], sem)
                        if step < 7:
                            z_copy(way, j, at, rows(step + 1, way, lo_row, n), 2 * gi + si, step + 1)
                        elif gi == 0 or way == si:
                            half = way * 64
                            z_copy(way, j, rows(7, way, half, 64), rows(0, 1, half, 64), 2 * gi + si, 8)
                        to_core(j, at)
                    elif gi == 0 or way == si:
                        at = rows(0, 1, way * 64, 64)
                        wait(wb.at[j, me, at, :], sem)
                        to_core(j, at)
            if step == 7 and gi == 0:
                for si, (j, lo_row, n) in enumerate(groups[1][0]):
                    for way in range(2):
                        z_copy(way, j, rows(0, 0, lo_row, n), rows(1, way, lo_row, n), 2 + si, 1)
            if step in tasks:
                tasks[step]()
    product(2, 0)
    product(2, 1)
    send_parts(2)

    wait(ssb.at[pl.ds(1, 7)], s_recv)
    total = ssb[0, 0:1, :]
    for r in range(1, 8):
        total = total + ssb[r, 0:1, :]
    scale_row = lax.rsqrt(total * (1.0 / D) + 1e-6)
    eye = lax.broadcasted_iota(jnp.int32, (TOK, TOK), 0) == lax.broadcasted_iota(jnp.int32, (TOK, TOK), 1)
    scale = jnp.sum(jnp.where(eye, scale_row, 0.0), axis=1, keepdims=True)

    def gathered(j):
        wait(rs.at[j, pl.ds(1, 7)], p_recv.at[j])
        own = ps[j, y_hi * 4 + x].astype(F32)
        for r in range(1, 4):
            own = own + rs[j, r].astype(F32)
        far = rs[j, 4].astype(F32)
        for r in range(5, 8):
            far = far + rs[j, r].astype(F32)
        return (
            jnp.where(y_hi == 0, own, far) * scale,
            jnp.where(y_hi == 0, far, own) * scale,
        )

    def rope(v):
        return (v * cos_t[...] + pltpu.roll(v, 64, 1) * sin_t[...]).astype(BF16)

    key, value = gathered(0)
    key = rope(key + bk_ref[...].astype(F32))
    value = (value + bv_ref[...].astype(F32)).astype(BF16)
    kv_t[:, 0:128] = key
    kv_t[:, 128:256] = value
    page_ref[...] = jnp.dot(hot_t[...], kv_t[...], preferred_element_type=F32).astype(BF16)

    def attend(head, q):
        q = rope(q + bq_ref[:, 128 * head : 128 * head + 128].astype(F32))
        s = lax.dot_general(q, kv_t[:, 0:128], nt, preferred_element_type=F32) * HD ** (-0.5) + mask_t[...]
        w = jnp.exp(s - jnp.max(s, axis=-1, keepdims=True))
        w = (w / jnp.sum(w, axis=-1, keepdims=True)).astype(BF16)
        att_ref[:, 128 * head : 128 * head + 128] = jnp.dot(
            w, kv_t[:, 128:256], preferred_element_type=F32
        ).astype(BF16)

    for j in (1, 2):
        low, high = gathered(j)
        attend(j - 1, low)
        attend(j + 1, high)

    wait(ws.at[pl.ds(0, 7)], ws_send)

    @pl.when(x != x_dst)
    def _():
        wait(ws.at[0], ws_send_self)

    wait(a5.at[pl.ds(0, 28)], h_send)
    wait(ssb.at[pl.ds(1, 7)], s_send)
    wait(wb.at[:, 0, pl.ds(0, 1920), :], z_send)
    wait(wb.at[:, 0], c_send)
    wait(rs.at[:, pl.ds(1, 7)], p_send)


def on_device(hidden, gain, wq, wk, wv, bq, bk, bv, lengths, table):
    vmem = pl.BlockSpec(memory_space=pltpu.VMEM)
    smem = pl.BlockSpec(memory_space=pltpu.SMEM)
    dma = pltpu.SemaphoreType.DMA
    att, pages = pl.pallas_call(
        kernel,
        out_shape=(
            jax.ShapeDtypeStruct((TOK, 4 * HD), BF16),
            jax.ShapeDtypeStruct((PAGES_REP * PAGE, 2 * HD), BF16),
        ),
        in_specs=[vmem] * 8 + [smem] * 2,
        out_specs=(vmem, vmem),
        scratch_shapes=[
            pltpu.VMEM((8, 3, 16, 256), BF16),
            pltpu.VMEM((3, 2, 2048, 256), BF16),
            pltpu.VMEM((2, 4, TOK, 128), BF16),
            pltpu.VMEM((32, TOK, 128), BF16),
            pltpu.VMEM((2, TOK, 2048), BF16),
            pltpu.VMEM((3, 8, TOK, 128), BF16),
            pltpu.VMEM((3, 8, TOK, 128), BF16),
            pltpu.VMEM((8, 8, TOK), F32),
            pltpu.VMEM((TOK, 128), F32),
            pltpu.VMEM((TOK, 128), F32),
            pltpu.VMEM((TOK, TOK), F32),
            pltpu.VMEM((PAGES_REP * PAGE, TOK), BF16),
            pltpu.VMEM((TOK, 256), BF16),
            dma, dma, dma, dma, dma((2, 4, 8)), dma, dma((3,)), dma, dma, dma, dma((3,)), dma, dma,
        ],
        compiler_params=pltpu.CompilerParams(
            collective_id=0, has_side_effects=True, vmem_limit_bytes=40 * 2**20
        ),
        name="handover",
    )(
        hidden, gain.reshape(64, 128), wq, wk, wv, bq.reshape(1, -1), bk.reshape(1, -1), bv.reshape(1, -1),
        lengths, table,
    )
    return att, pages.reshape(PAGES_REP, PAGE, 2 * HD)


def solution(mesh):
    placed = (
        P("dp", "tensor"),
        P(),
        P(("dp", "tensor"), None),
        P(("dp", "tensor"), None),
        P(("dp", "tensor"), None),
        P("tensor"),
        P("tensor"),
        P("tensor"),
        P("dp", None),
        P("dp", None),
    )
    return jax.shard_map(
        on_device,
        mesh=mesh,
        in_specs=placed,
        out_specs=(P("dp", "tensor"), P("dp", None, "tensor")),
        check_vma=False,
    )
```

```python
import functools
import math

import jax
import jax.numpy as jnp
from jax import lax
from jax.experimental import pallas as pl
from jax.experimental.pallas import tpu as pltpu
from jax.sharding import PartitionSpec as P

MESH = pl.DeviceIdType.MESH
HD = 128
ROLLS = 4
PAGE = 32
BLOCKS = 4
PAGES_REP = 16
TOK = 256
D = 8192
NZ = 16
BASE = 1000000.0
F32 = jnp.float32
BF16 = jnp.bfloat16
NEG = -1e30
LATE = (0, 0, 3)
SPLIT = (2, 2, 4)


def rem(a, n):
    return lax.rem(a, n)


def kernel(
    h_in, gain_in, wq_in, wk_in, wv_in, bq_in, bk_in, bv_in, len_ref, pt_ref,
    att_ref, page_ref,
    h_ref, gain_ref, wq_ref, wk_ref, wv_ref, bq_ref, bk_ref, bv_ref, in_sem,
    ws, wb, hs, a5, a2, ps, rs, ssb, cos_t, sin_t, mask_t, hot_t, kv_t,
    ws_send, ws_send_self, ws_recv, z_send, z_recv, c_send, c_recv, h_send, h_recv, p_send, p_recv, s_send, s_recv,
):
    dp = lax.axis_index("dp")
    t = lax.axis_index("tensor")
    y_hi, z, core = dp // (2 * NZ), rem(dp // 2, NZ), rem(dp, 2)
    x, y_lo = t // 2, rem(t, 2)

    def dev(x, y_lo, y_hi, z, core):
        return ((y_hi * NZ + z) * 2 + core, x * 2 + y_lo)

    def flip(bit, by):
        return rem(bit + by, 2)

    def bring(i):
        src = (gain_in, wq_in, wk_in, wv_in, h_in, bq_in, bk_in, bv_in)[i]
        dst = (gain_ref, wq_ref, wk_ref, wv_ref, h_ref, bq_ref, bk_ref, bv_ref)[i]
        return pltpu.make_async_copy(src, dst, in_sem.at[i])

    for i in range(8):
        bring(i).start()

    barrier = pltpu.get_barrier_semaphore()
    peers = []
    for r in range(1, 32):
        peers.append(dev(rem(x + r % 4, 4), flip(y_lo, r // 4 % 2), flip(y_hi, r // 8 % 2), z, flip(core, r // 16)))
    up, down = rem(z + 1, NZ), rem(z + NZ - 1, NZ)
    up_dev, down_dev = dev(x, y_lo, y_hi, up, core), dev(x, y_lo, y_hi, down, core)
    peers += [up_dev, down_dev]
    for d in peers:
        pl.semaphore_signal(barrier, inc=1, device_id=d, device_id_type=MESH)

    for i in range(4):
        bring(i).wait()
    g = gain_ref[...].astype(F32)
    g_row = jnp.sum(jnp.where(lax.broadcasted_iota(jnp.int32, g.shape, 0) == dp, g, 0.0), axis=0, keepdims=True)
    lane = lax.broadcasted_iota(jnp.int32, (16, 128), 1)
    sub = lax.broadcasted_iota(jnp.int32, (16, 128), 0)
    g_col = jnp.sum(jnp.where(lane == sub + 16 * t, g_row, 0.0), axis=1, keepdims=True)
    for yh_d in range(2):
        for yl_d in range(2):
            for k in range(2):
                for e in range(2):
                    td = 4 * k + 2 * e + yl_d
                    first = (wk_ref if yh_d == 0 else wv_ref)[:, 128 * td : 128 * td + 128]
                    q0 = 512 * td + 256 * yh_d
                    parts = (first, wq_ref[:, q0 : q0 + 128], wq_ref[:, q0 + 128 : q0 + 256])
                    for j in range(3):
                        ws[(yh_d * 2 + yl_d) * 2 + k, j, :, 128 * e : 128 * e + 128] = (
                            parts[j].astype(F32) * g_col
                        ).astype(BF16)
    for i in range(4, 8):
        bring(i).wait()
    for b in range(2):
        for u in range(4):
            hs[b, u] = h_ref[:, 256 * u + 128 * b : 256 * u + 128 * b + 128]

    pl.semaphore_wait(barrier, len(peers))

    def remote(src, dst, send, recv, device):
        pltpu.make_async_remote_copy(
            src_ref=src, dst_ref=dst, send_sem=send, recv_sem=recv, device_id=device, device_id_type=MESH
        ).start()

    def wait(ref, sem):
        pltpu.make_async_copy(ref, ref, sem).wait()

    x_dst = 2 * y_hi + core
    slot_w = pl.ds(pl.multiple_of(16 * t, 16), 16)
    for r in range(8):
        yl_d, yh_d, k = flip(y_lo, r % 2), flip(y_hi, r // 2 % 2), flip(core, r // 4)
        src = ws.at[(yh_d * 2 + yl_d) * 2 + k]
        dst = wb.at[:, k, slot_w, :]
        to = dev(x_dst, yl_d, yh_d, z, k)
        if r > 0:
            remote(src, dst, ws_send, ws_recv, to)
        else:

            @pl.when(x == x_dst)
            def _():
                pltpu.make_async_copy(src, dst, ws_recv).start()

            @pl.when(x != x_dst)
            def _():
                remote(src, dst, ws_send_self, ws_recv, to)

    xb = rem(x, 2)
    x_pair = x + 1 - 2 * xb
    piece = 4 * (y_hi * 4 + rem(t, 4))
    for r in (1, 2, 3, 4, 5, 6, 7):
        xd = x if r < 4 else x_pair
        src = hs.at[xb if r < 4 else 1 - xb]
        to = dev(xd, flip(y_lo, r % 2), flip(y_hi, r // 2 % 2), z, core)
        remote(src, a5.at[pl.ds(piece, 4)], h_send, h_recv, to)
    for u in range(4):
        a5[piece + u] = hs[xb, u]

    me = core
    other = 1 - core

    def rows(p, half, lo=0, n=128):
        return pl.ds(p * 256 + half * 128 + lo, n)

    def z_copy(way, j, src_rows, dst_rows, sub_id, step):
        remote(
            wb.at[j, me, src_rows, :], wb.at[j, me, dst_rows, :], z_send, z_recv.at[way, sub_id, step - 1],
            up_dev if way == 0 else down_dev,
        )

    def to_core(j, at):
        remote(wb.at[j, me, at, :], wb.at[j, me, at, :], c_send, c_recv.at[j], dev(x, y_lo, y_hi, z, other))

    wait(wb.at[:, me, rows(0, 0), :], ws_recv)
    subs = []
    for j in range(3):
        n = 128 // SPLIT[j]
        subs += [(j, n * q, n) for q in range(SPLIT[j])]

    def own(cycle):
        for si, (j, lo_row, n) in enumerate(subs):
            if LATE[j] == cycle:
                for way in range(2):
                    z_copy(way, j, rows(0, 0, lo_row, n), rows(1, way, lo_row, n), si, 1)

    own(0)

    h = h_ref[...].astype(F32)
    sq = h * h
    hi = sq.astype(BF16)
    lo = (sq - hi.astype(F32)).astype(BF16)
    ones = jnp.ones((8, 1024), BF16)
    nt = (((1,), (1,)), ((), ()))
    ssb[0] = lax.dot_general(ones, hi, nt, preferred_element_type=F32) + lax.dot_general(
        ones, lo, nt, preferred_element_type=F32
    )
    for r in range(1, 8):
        remote(ssb.at[0], ssb.at[r], s_send, s_recv, dev(rem(x + r % 4, 4), flip(y_lo, r // 4), y_hi, z, core))
    for j in range(3):
        to_core(j, rows(0, 0))

    def first_tables():
        ends, starts, total = [], [], 0
        for r in range(ROLLS):
            starts.append(total)
            total = total + len_ref[0, r]
            ends.append(total)
        tok = lax.broadcasted_iota(jnp.int32, (TOK, 128), 0)
        begin = jnp.zeros((TOK, 128), jnp.int32)
        for r in range(1, ROLLS):
            begin = jnp.where(tok >= ends[r - 1], starts[r], begin)
        d = lax.broadcasted_iota(jnp.int32, (TOK, 128), 1)
        half = rem(d, 64).astype(F32)
        freq = jnp.exp(half * (-2.0 / HD * math.log(BASE)))
        angle = (tok - begin).astype(F32) * freq
        cos_t[...] = jnp.cos(angle)
        s = jnp.sin(angle)
        sin_t[...] = jnp.where(d < 64, -s, s)
        for q in range(2):
            col = d + 128 * q
            mask_t[:, 128 * q : 128 * q + 128] = jnp.where((col >= begin) & (col <= tok), 0.0, NEG)

    def page_tables():
        ends, starts, total = [], [], 0
        for r in range(ROLLS):
            starts.append(total)
            total = total + len_ref[0, r]
        n = lax.broadcasted_iota(jnp.int32, (PAGES_REP * PAGE, 128), 0)
        page, slot = n // PAGE, rem(n, PAGE)
        src = jnp.full(n.shape, -1, jnp.int32)
        for e in range(PAGES_REP):
            r, b = e // BLOCKS, e % BLOCKS
            at = b * PAGE + slot
            src = jnp.where((page == pt_ref[0, e]) & (at < len_ref[0, r]), starts[r] + at, src)
        col = lax.broadcasted_iota(jnp.int32, (PAGES_REP * PAGE, 128), 1)
        for q in range(2):
            hot_t[:, 128 * q : 128 * q + 128] = jnp.where(src == col + 128 * q, 1.0, 0.0).astype(BF16)

    def wait_hidden():
        wait(a5.at[pl.ds(0, 28)], h_recv)

    def relay(tk):
        for p in range(8):
            m1 = rem(z + NZ - p, NZ)
            m2 = rem(z + p, NZ) if p else rem(z + 8, NZ)
            a2[tk, :, 256 * p : 256 * p + 128] = a5[tk * NZ + m1]
            a2[tk, :, 256 * p + 128 : 256 * p + 256] = a5[tk * NZ + m2]

    def product(j, k):
        if k == 0:
            wait(wb.at[j, other], c_recv.at[j])

        @pl.loop(0, 2)
        def _(tk):
            part = jnp.dot(a2[tk], wb[j, k], preferred_element_type=F32).astype(BF16)
            for e in range(2):
                ps[j, tk * 4 + 2 * k + e] = part[:, 128 * e : 128 * e + 128]

    def send_parts(j):
        for r in range(7, 0, -1):
            xd, yh_d = rem(x + r % 4, 4), flip(y_hi, r // 4)
            remote(ps.at[j, yh_d * 4 + xd], rs.at[j, r], p_send, p_recv.at[j], dev(xd, y_lo, yh_d, z, core))

    def both(tasks):
        def run():
            for f in tasks:
                f()

        return run

    P_ = functools.partial
    tasks = {1: [first_tables], 3: [page_tables], 6: [wait_hidden, P_(relay, 0)], 7: [P_(relay, 1)]}
    last = max(LATE) + 8
    queue = []
    for cycle in range(1, last + 1):
        for si, (j, lo_row, n) in enumerate(subs):
            step = cycle - LATE[j]
            if not 1 <= step <= 8:
                continue
            half = n // 2
            for way in range(2):
                sem = z_recv.at[way, si, step - 1]
                lo2 = lo_row + way * half
                if step < 8:
                    at = rows(step, way, lo_row, n)
                    wait(wb.at[j, me, at, :], sem)
                    if step < 7:
                        z_copy(way, j, at, rows(step + 1, way, lo_row, n), si, step + 1)
                    else:
                        z_copy(way, j, rows(7, way, lo2, half), rows(0, 1, lo2, half), si, 8)
                else:
                    wait(wb.at[j, me, rows(0, 1, lo2, half), :], sem)
        own(cycle)
        for j in range(3):
            step = cycle - LATE[j]
            if 1 <= step < 8:
                for way in range(2):
                    to_core(j, rows(step, way))
            if step == 8:
                to_core(j, rows(0, 1))
                queue += [P_(product, j, 0), both([P_(product, j, 1), P_(send_parts, j)])]
        if cycle in tasks:
            for f in tasks[cycle]:
                f()
        elif cycle < last:
            for _ in range(min(2, len(queue))):
                queue.pop(0)()
    for f in queue:
        f()

    wait(ssb.at[pl.ds(1, 7)], s_recv)
    total = ssb[0, 0:1, :]
    for r in range(1, 8):
        total = total + ssb[r, 0:1, :]
    scale_row = lax.rsqrt(total * (1.0 / D) + 1e-6)
    eye = lax.broadcasted_iota(jnp.int32, (TOK, TOK), 0) == lax.broadcasted_iota(jnp.int32, (TOK, TOK), 1)
    scale = jnp.sum(jnp.where(eye, scale_row, 0.0), axis=1, keepdims=True)

    def gathered(j):
        wait(rs.at[j, pl.ds(1, 7)], p_recv.at[j])
        own = ps[j, y_hi * 4 + x].astype(F32)
        for r in range(1, 4):
            own = own + rs[j, r].astype(F32)
        far = rs[j, 4].astype(F32)
        for r in range(5, 8):
            far = far + rs[j, r].astype(F32)
        return (
            jnp.where(y_hi == 0, own, far) * scale,
            jnp.where(y_hi == 0, far, own) * scale,
        )

    def rope(v):
        return (v * cos_t[...] + pltpu.roll(v, 64, 1) * sin_t[...]).astype(BF16)

    key, value = gathered(0)
    key = rope(key + bk_ref[...].astype(F32))
    value = (value + bv_ref[...].astype(F32)).astype(BF16)
    kv_t[:, 0:128] = key
    kv_t[:, 128:256] = value
    page_ref[...] = jnp.dot(hot_t[...], kv_t[...], preferred_element_type=F32).astype(BF16)

    def attend(head, q):
        q = rope(q + bq_ref[head : head + 1].astype(F32))
        s = lax.dot_general(q, kv_t[:, 0:128], nt, preferred_element_type=F32) * HD ** (-0.5) + mask_t[...]
        w = jnp.exp(s - jnp.max(s, axis=-1, keepdims=True))
        w = (w / jnp.sum(w, axis=-1, keepdims=True)).astype(BF16)
        att_ref[:, 128 * head : 128 * head + 128] = jnp.dot(
            w, kv_t[:, 128:256], preferred_element_type=F32
        ).astype(BF16)

    for j in (1, 2):
        low, high = gathered(j)
        attend(j - 1, low)
        attend(j + 1, high)

    wait(ws.at[pl.ds(0, 7)], ws_send)

    @pl.when(x != x_dst)
    def _():
        wait(ws.at[0], ws_send_self)

    wait(a5.at[pl.ds(0, 28)], h_send)
    wait(ssb.at[pl.ds(1, 7)], s_send)
    wait(wb.at[:, 0, pl.ds(0, 1920), :], z_send)
    wait(wb.at[:, 0], c_send)
    wait(rs.at[:, pl.ds(1, 7)], p_send)


def on_device(hidden, gain, wq, wk, wv, bq, bk, bv, lengths, table):
    hbm = pl.BlockSpec(memory_space=pltpu.MemorySpace.HBM)
    vmem = pl.BlockSpec(memory_space=pltpu.VMEM)
    smem = pl.BlockSpec(memory_space=pltpu.SMEM)
    dma = pltpu.SemaphoreType.DMA
    att, pages = pl.pallas_call(
        kernel,
        out_shape=(
            jax.ShapeDtypeStruct((TOK, 4 * HD), BF16),
            jax.ShapeDtypeStruct((PAGES_REP * PAGE, 2 * HD), BF16),
        ),
        in_specs=[hbm] * 8 + [smem] * 2,
        out_specs=(vmem, vmem),
        scratch_shapes=[
            *[
                pltpu.VMEM(s, BF16)
                for s in ((TOK, 1024), (64, 128), (16, 4096), (16, 1024), (16, 1024), (4, 128), (1, 128), (1, 128))
            ],
            dma((8,)),
            pltpu.VMEM((8, 3, 16, 256), BF16),
            pltpu.VMEM((3, 2, 2048, 256), BF16),
            pltpu.VMEM((2, 4, TOK, 128), BF16),
            pltpu.VMEM((32, TOK, 128), BF16),
            pltpu.VMEM((2, TOK, 2048), BF16),
            pltpu.VMEM((3, 8, TOK, 128), BF16),
            pltpu.VMEM((3, 8, TOK, 128), BF16),
            pltpu.VMEM((8, 8, TOK), F32),
            pltpu.VMEM((TOK, 128), F32),
            pltpu.VMEM((TOK, 128), F32),
            pltpu.VMEM((TOK, TOK), F32),
            pltpu.VMEM((PAGES_REP * PAGE, TOK), BF16),
            pltpu.VMEM((TOK, 256), BF16),
            dma, dma, dma, dma, dma((2, 8, 8)), dma, dma((3,)), dma, dma, dma, dma((3,)), dma, dma,
        ],
        compiler_params=pltpu.CompilerParams(
            collective_id=0, has_side_effects=True, vmem_limit_bytes=60 * 2**20
        ),
        name="handover",
    )(
        hidden, gain.reshape(64, 128), wq, wk, wv, bq.reshape(4, -1), bk.reshape(1, -1), bv.reshape(1, -1),
        lengths, table,
    )
    return att, pages.reshape(PAGES_REP, PAGE, 2 * HD)


def solution(mesh):
    placed = (
        P("dp", "tensor"),
        P(),
        P(("dp", "tensor"), None),
        P(("dp", "tensor"), None),
        P(("dp", "tensor"), None),
        P("tensor"),
        P("tensor"),
        P("tensor"),
        P("dp", None),
        P("dp", None),
    )
    return jax.shard_map(
        on_device,
        mesh=mesh,
        in_specs=placed,
        out_specs=(P("dp", "tensor"), P("dp", None, "tensor")),
        check_vma=False,
    )
```

```python
import functools
import math

import jax
import jax.numpy as jnp
from jax import lax
from jax.experimental import pallas as pl
from jax.experimental.pallas import tpu as pltpu
from jax.sharding import PartitionSpec as P

MESH = pl.DeviceIdType.MESH
HD = 128
ROLLS = 4
PAGE = 32
BLOCKS = 4
PAGES_REP = 16
TOK = 256
D = 8192
NZ = 16
BASE = 1000000.0
F32 = jnp.float32
BF16 = jnp.bfloat16
NEG = -1e30
LATE = (0, 0, 3)
SPLIT = (2, 2, 4)
U = 3


def rem(a, n):
    return lax.rem(a, n)


def kernel(
    h_in, gain_in, wq_in, wk_in, wv_in, bq_in, bk_in, bv_in, len_ref, pt_ref,
    att_ref, page_ref,
    h_ref, gain_ref, wq_ref, wk_ref, wv_ref, bq_ref, bk_ref, bv_ref, in_sem,
    ws, wb, a5, a2, ps, rs, ssb, cos_t, sin_t, mask_t, hot_t, kv_t,
    ws_send, ws_send_self, ws_recv, z_send, z_recv, c_send, c_recv, h_send, h_recv, p_send, p_recv, s_send, s_recv,
):
    dp = lax.axis_index("dp")
    t = lax.axis_index("tensor")
    y_hi, z, core = dp // (2 * NZ), rem(dp // 2, NZ), rem(dp, 2)
    x, y_lo = t // 2, rem(t, 2)

    def dev(x, y_lo, y_hi, z, core):
        return ((y_hi * NZ + z) * 2 + core, x * 2 + y_lo)

    def flip(bit, by):
        return rem(bit + by, 2)

    def bring(i):
        src = (gain_in, wq_in, wk_in, wv_in, h_in, bq_in, bk_in, bv_in)[i]
        dst = (gain_ref, wq_ref, wk_ref, wv_ref, h_ref, bq_ref, bk_ref, bv_ref)[i]
        return pltpu.make_async_copy(src, dst, in_sem.at[i])

    for i in range(8):
        bring(i).start()

    barrier = pltpu.get_barrier_semaphore()
    peers = []
    for r in range(1, 32):
        peers.append(dev(rem(x + r % 4, 4), flip(y_lo, r // 4 % 2), flip(y_hi, r // 8 % 2), z, flip(core, r // 16)))
    up, down = rem(z + 1, NZ), rem(z + NZ - 1, NZ)
    up_dev, down_dev = dev(x, y_lo, y_hi, up, core), dev(x, y_lo, y_hi, down, core)
    peers += [up_dev, down_dev]
    for d in peers:
        pl.semaphore_signal(barrier, inc=1, device_id=d, device_id_type=MESH)

    for i in range(4):
        bring(i).wait()
    g = gain_ref[...].astype(F32)
    g_row = jnp.sum(jnp.where(lax.broadcasted_iota(jnp.int32, g.shape, 0) == dp, g, 0.0), axis=0, keepdims=True)
    lane = lax.broadcasted_iota(jnp.int32, (16, 128), 1)
    sub = lax.broadcasted_iota(jnp.int32, (16, 128), 0)
    g_col = jnp.sum(jnp.where(lane == sub + 16 * t, g_row, 0.0), axis=1, keepdims=True)
    for yh_d in range(2):
        for yl_d in range(2):
            for k in range(2):
                for e in range(2):
                    td = 4 * e + 2 * k + yl_d
                    first = (wk_ref if yh_d == 0 else wv_ref)[:, 128 * td : 128 * td + 128]
                    q0 = 512 * td + 256 * yh_d
                    parts = (first, wq_ref[:, q0 : q0 + 128], wq_ref[:, q0 + 128 : q0 + 256])
                    for j in range(3):
                        ws[(yh_d * 2 + yl_d) * 2 + k, j, :, 128 * e : 128 * e + 128] = (
                            parts[j].astype(F32) * g_col
                        ).astype(BF16)
    for i in range(4, 8):
        bring(i).wait()
    x0, x1 = rem(x, 2), x // 2
    piece = (y_hi * 4 + rem(t, 4)) * 8
    for u in range(8):
        a5[piece + u] = h_ref[:, 128 * u : 128 * u + 128]

    pl.semaphore_wait(barrier, len(peers))

    def remote(src, dst, send, recv, device):
        pltpu.make_async_remote_copy(
            src_ref=src, dst_ref=dst, send_sem=send, recv_sem=recv, device_id=device, device_id_type=MESH
        ).start()

    def wait(ref, sem):
        pltpu.make_async_copy(ref, ref, sem).wait()

    slot_w = pl.ds(pl.multiple_of(16 * t, 16), 16)
    for r in range(8):
        yl_d, yh_d, k = flip(y_lo, r % 2), flip(y_hi, r // 2 % 2), flip(x0, r // 4)
        src = ws.at[(yh_d * 2 + yl_d) * 2 + k]
        dst = wb.at[:, core, slot_w, :]
        to = dev(2 * y_hi + k, yl_d, yh_d, z, core)
        if r > 0:
            remote(src, dst, ws_send, ws_recv, to)
        else:

            @pl.when(x1 == y_hi)
            def _():
                pltpu.make_async_copy(src, dst, ws_recv).start()

            @pl.when(x1 != y_hi)
            def _():
                remote(src, dst, ws_send_self, ws_recv, to)

    pair = dev(2 * x1 + 1 - x0, y_lo, y_hi, z, core)
    pair_piece = (y_hi * 4 + 2 * (1 - x0) + y_lo) * 8

    def row(r):
        return flip(y_lo, r % 2), flip(y_hi, r // 2)

    def move(base, lo, n, sem, to):
        at = a5.at[pl.ds(base + lo, n)]
        remote(at, at, h_send, h_recv.at[sem], to)

    def own_x(lo, n, sem):
        move(piece, lo, n, sem, pair)

    def own_y(r, lo, n, sem):
        yl, yh = row(r)
        move(piece, lo, n, sem, dev(x, yl, yh, z, core))

    def pair_y(r):
        yl, yh = row(r)
        move(pair_piece, 0, U, 5, dev(x, yl, yh, z, core))

    def got(n, sem):
        wait(a5.at[pl.ds(0, n)], h_recv.at[sem])

    def pass_x(r):
        got(8 - U, 1 + r)
        yl, yh = row(r)
        move((yh * 4 + 2 * x0 + yl) * 8, U, 8 - U, 7, pair)

    own_x(0, U, 0)
    for r in (1, 3):
        own_y(r, U, 8 - U, 1 + r)

    def hidden_0():
        own_x(U, 8 - U, 1)
        got(U, 0)
        pair_y(1)
        pair_y(3)

    def hidden_1():
        own_y(2, U, 8 - U, 3)
        pass_x(1)
        pass_x(3)

    def hidden_2():
        own_y(1, 0, U, 6)
        own_y(3, 0, U, 6)

    def hidden_4():
        own_y(2, 0, U, 6)
        pair_y(2)
        pass_x(2)

    def wait_hidden():
        got(8 - U, 1)
        got(3 * U, 5)
        got(3 * U, 6)
        got(3 * (8 - U), 7)

    me = core
    other = 1 - core

    def rows(p, half, lo=0, n=128):
        return pl.ds(p * 256 + half * 128 + lo, n)

    def z_copy(way, j, src_rows, dst_rows, sub_id, step):
        remote(
            wb.at[j, me, src_rows, :], wb.at[j, me, dst_rows, :], z_send, z_recv.at[way, sub_id, step - 1],
            up_dev if way == 0 else down_dev,
        )

    def to_core(j, at):
        remote(wb.at[j, me, at, :], wb.at[j, me, at, :], c_send, c_recv.at[j], dev(x, y_lo, y_hi, z, other))

    wait(wb.at[:, me, rows(0, 0), :], ws_recv)
    subs = []
    for j in range(3):
        n = 128 // SPLIT[j]
        subs += [(j, n * q, n) for q in range(SPLIT[j])]

    def own(cycle):
        for si, (j, lo_row, n) in enumerate(subs):
            if LATE[j] == cycle:
                for way in range(2):
                    z_copy(way, j, rows(0, 0, lo_row, n), rows(1, way, lo_row, n), si, 1)

    own(0)
    hidden_0()

    h = h_ref[...].astype(F32)
    sq = h * h
    hi = sq.astype(BF16)
    lo = (sq - hi.astype(F32)).astype(BF16)
    ones = jnp.ones((8, 1024), BF16)
    nt = (((1,), (1,)), ((), ()))
    ssb[0] = lax.dot_general(ones, hi, nt, preferred_element_type=F32) + lax.dot_general(
        ones, lo, nt, preferred_element_type=F32
    )
    for r in range(1, 8):
        remote(ssb.at[0], ssb.at[r], s_send, s_recv, dev(rem(x + r % 4, 4), flip(y_lo, r // 4), y_hi, z, core))
    for j in range(3):
        to_core(j, rows(0, 0))

    def first_tables():
        ends, starts, total = [], [], 0
        for r in range(ROLLS):
            starts.append(total)
            total = total + len_ref[0, r]
            ends.append(total)
        tok = lax.broadcasted_iota(jnp.int32, (TOK, 128), 0)
        begin = jnp.zeros((TOK, 128), jnp.int32)
        for r in range(1, ROLLS):
            begin = jnp.where(tok >= ends[r - 1], starts[r], begin)
        d = lax.broadcasted_iota(jnp.int32, (TOK, 128), 1)
        half = rem(d, 64).astype(F32)
        freq = jnp.exp(half * (-2.0 / HD * math.log(BASE)))
        angle = (tok - begin).astype(F32) * freq
        cos_t[...] = jnp.cos(angle)
        s = jnp.sin(angle)
        sin_t[...] = jnp.where(d < 64, -s, s)
        for q in range(2):
            col = d + 128 * q
            mask_t[:, 128 * q : 128 * q + 128] = jnp.where((col >= begin) & (col <= tok), 0.0, NEG)

    def page_tables():
        ends, starts, total = [], [], 0
        for r in range(ROLLS):
            starts.append(total)
            total = total + len_ref[0, r]
        n = lax.broadcasted_iota(jnp.int32, (PAGES_REP * PAGE, 128), 0)
        page, slot = n // PAGE, rem(n, PAGE)
        src = jnp.full(n.shape, -1, jnp.int32)
        for e in range(PAGES_REP):
            r, b = e // BLOCKS, e % BLOCKS
            at = b * PAGE + slot
            src = jnp.where((page == pt_ref[0, e]) & (at < len_ref[0, r]), starts[r] + at, src)
        col = lax.broadcasted_iota(jnp.int32, (PAGES_REP * PAGE, 128), 1)
        for q in range(2):
            hot_t[:, 128 * q : 128 * q + 128] = jnp.where(src == col + 128 * q, 1.0, 0.0).astype(BF16)

    def relay(tk, k):
        for p in range(8):
            m1 = rem(z + NZ - p, NZ)
            m2 = rem(z + p, NZ) if p else rem(z + 8, NZ)
            a2[tk, k, :, 256 * p : 256 * p + 128] = a5[tk * 32 + 2 * m1 + k]
            a2[tk, k, :, 256 * p + 128 : 256 * p + 256] = a5[tk * 32 + 2 * m2 + k]

    def product(j, far):
        tk = 1 - y_hi if far else y_hi
        if far:
            wait(wb.at[j, other], c_recv.at[j])
        part = jnp.dot(a2[tk, 0], wb[j, 0], preferred_element_type=F32) + jnp.dot(
            a2[tk, 1], wb[j, 1], preferred_element_type=F32
        )
        part = part.astype(BF16)
        for e in range(2):
            ps[j, tk * 2 + e] = part[:, 128 * e : 128 * e + 128]
        for r in (3, 2) if far else (1,):
            e = flip(x1, r % 2)
            remote(
                ps.at[j, tk * 2 + e], rs.at[j, r], p_send, p_recv.at[j], dev(2 * e + x0, y_lo, tk, z, core)
            )

    P_ = functools.partial
    tasks = {
        1: [hidden_1], 2: [hidden_2, first_tables], 3: [page_tables], 4: [hidden_4],
        7: [wait_hidden, P_(relay, 0, 0), P_(relay, 0, 1)], 8: [P_(relay, 1, 0), P_(relay, 1, 1)],
    }
    last = max(LATE) + 8
    queue = []
    for cycle in range(1, last + 1):
        for si, (j, lo_row, n) in enumerate(subs):
            step = cycle - LATE[j]
            if not 1 <= step <= 8:
                continue
            half = n // 2
            for way in range(2):
                sem = z_recv.at[way, si, step - 1]
                lo2 = lo_row + way * half
                if step < 8:
                    at = rows(step, way, lo_row, n)
                    wait(wb.at[j, me, at, :], sem)
                    if step < 7:
                        z_copy(way, j, at, rows(step + 1, way, lo_row, n), si, step + 1)
                    else:
                        z_copy(way, j, rows(7, way, lo2, half), rows(0, 1, lo2, half), si, 8)
                else:
                    wait(wb.at[j, me, rows(0, 1, lo2, half), :], sem)
        own(cycle)
        for j in range(3):
            step = cycle - LATE[j]
            if 1 <= step < 8:
                for way in range(2):
                    to_core(j, rows(step, way))
            if step == 8:
                to_core(j, rows(0, 1))
                queue += [P_(product, j, True), P_(product, j, False)]
        if cycle in tasks:
            for f in tasks[cycle]:
                f()
        elif cycle < last:
            for _ in range(min(2, len(queue))):
                queue.pop(0)()
    for f in queue:
        f()

    wait(ssb.at[pl.ds(1, 7)], s_recv)
    total = ssb[0, 0:1, :]
    for r in range(1, 8):
        total = total + ssb[r, 0:1, :]
    scale_row = lax.rsqrt(total * (1.0 / D) + 1e-6)
    eye = lax.broadcasted_iota(jnp.int32, (TOK, TOK), 0) == lax.broadcasted_iota(jnp.int32, (TOK, TOK), 1)
    scale = jnp.sum(jnp.where(eye, scale_row, 0.0), axis=1, keepdims=True)

    def gathered(j):
        wait(rs.at[j, pl.ds(1, 3)], p_recv.at[j])
        own = ps[j, y_hi * 2 + x1].astype(F32) + rs[j, 1].astype(F32)
        far = rs[j, 2].astype(F32) + rs[j, 3].astype(F32)
        return (
            jnp.where(y_hi == 0, own, far) * scale,
            jnp.where(y_hi == 0, far, own) * scale,
        )

    def rope(v):
        return (v * cos_t[...] + pltpu.roll(v, 64, 1) * sin_t[...]).astype(BF16)

    key, value = gathered(0)
    key = rope(key + bk_ref[...].astype(F32))
    value = (value + bv_ref[...].astype(F32)).astype(BF16)
    kv_t[:, 0:128] = key
    kv_t[:, 128:256] = value
    page_ref[...] = jnp.dot(hot_t[...], kv_t[...], preferred_element_type=F32).astype(BF16)

    def attend(head, q):
        q = rope(q + bq_ref[head : head + 1].astype(F32))
        s = lax.dot_general(q, kv_t[:, 0:128], nt, preferred_element_type=F32) * HD ** (-0.5) + mask_t[...]
        w = jnp.exp(s - jnp.max(s, axis=-1, keepdims=True))
        w = (w / jnp.sum(w, axis=-1, keepdims=True)).astype(BF16)
        att_ref[:, 128 * head : 128 * head + 128] = jnp.dot(
            w, kv_t[:, 128:256], preferred_element_type=F32
        ).astype(BF16)

    for j in (1, 2):
        low, high = gathered(j)
        attend(j - 1, low)
        attend(j + 1, high)

    wait(ws.at[pl.ds(0, 7)], ws_send)

    @pl.when(x1 != y_hi)
    def _():
        wait(ws.at[0], ws_send_self)

    wait(a5.at[pl.ds(0, 56)], h_send)
    wait(ssb.at[pl.ds(1, 7)], s_send)
    wait(wb.at[:, 0, pl.ds(0, 1920), :], z_send)
    wait(wb.at[:, 0], c_send)
    wait(rs.at[:, pl.ds(1, 3)], p_send)


def on_device(hidden, gain, wq, wk, wv, bq, bk, bv, lengths, table):
    hbm = pl.BlockSpec(memory_space=pltpu.MemorySpace.HBM)
    vmem = pl.BlockSpec(memory_space=pltpu.VMEM)
    smem = pl.BlockSpec(memory_space=pltpu.SMEM)
    dma = pltpu.SemaphoreType.DMA
    att, pages = pl.pallas_call(
        kernel,
        out_shape=(
            jax.ShapeDtypeStruct((TOK, 4 * HD), BF16),
            jax.ShapeDtypeStruct((PAGES_REP * PAGE, 2 * HD), BF16),
        ),
        in_specs=[hbm] * 8 + [smem] * 2,
        out_specs=(vmem, vmem),
        scratch_shapes=[
            *[
                pltpu.VMEM(s, BF16)
                for s in ((TOK, 1024), (64, 128), (16, 4096), (16, 1024), (16, 1024), (4, 128), (1, 128), (1, 128))
            ],
            dma((8,)),
            pltpu.VMEM((8, 3, 16, 256), BF16),
            pltpu.VMEM((3, 2, 2048, 256), BF16),
            pltpu.VMEM((64, TOK, 128), BF16),
            pltpu.VMEM((2, 2, TOK, 2048), BF16),
            pltpu.VMEM((3, 4, TOK, 128), BF16),
            pltpu.VMEM((3, 4, TOK, 128), BF16),
            pltpu.VMEM((8, 8, TOK), F32),
            pltpu.VMEM((TOK, 128), F32),
            pltpu.VMEM((TOK, 128), F32),
            pltpu.VMEM((TOK, TOK), F32),
            pltpu.VMEM((PAGES_REP * PAGE, TOK), BF16),
            pltpu.VMEM((TOK, 256), BF16),
            dma, dma, dma, dma, dma((2, 8, 8)), dma, dma((3,)), dma, dma((8,)), dma, dma((3,)), dma, dma,
        ],
        compiler_params=pltpu.CompilerParams(
            collective_id=0, has_side_effects=True, vmem_limit_bytes=60 * 2**20
        ),
        name="handover",
    )(
        hidden, gain.reshape(64, 128), wq, wk, wv, bq.reshape(4, -1), bk.reshape(1, -1), bv.reshape(1, -1),
        lengths, table,
    )
    return att, pages.reshape(PAGES_REP, PAGE, 2 * HD)


def solution(mesh):
    placed = (
        P("dp", "tensor"),
        P(),
        P(("dp", "tensor"), None),
        P(("dp", "tensor"), None),
        P(("dp", "tensor"), None),
        P("tensor"),
        P("tensor"),
        P("tensor"),
        P("dp", None),
        P("dp", None),
    )
    return jax.shard_map(
        on_device,
        mesh=mesh,
        in_specs=placed,
        out_specs=(P("dp", "tensor"), P("dp", None, "tensor")),
        check_vma=False,
    )
```

```python
import functools
import math

import jax
import jax.numpy as jnp
from jax import lax
from jax.experimental import pallas as pl
from jax.experimental.pallas import tpu as pltpu
from jax.sharding import PartitionSpec as P

MESH = pl.DeviceIdType.MESH
HD = 128
ROLLS = 4
PAGE = 32
BLOCKS = 4
PAGES_REP = 16
TOK = 256
D = 8192
NZ = 16
BASE = 1000000.0
F32 = jnp.float32
BF16 = jnp.bfloat16
NEG = -1e30
LATE = (0, 1, 1)
SPLIT = (2, 2, 2)
WH = 7
U = 3


def rem(a, n):
    return lax.rem(a, n)


def kernel(
    h_in, gain_in, wq_in, wk_in, wv_in, bq_in, bk_in, bv_in, len_ref, pt_ref,
    att_ref, page_ref,
    h_ref, gain_ref, wq_ref, wk_ref, wv_ref, bq_ref, bk_ref, bv_ref, in_sem,
    ws, wb, a5, a2, ps, rs, ssb, cos_t, sin_t, mask_t, hot_t, kv_t,
    ws_send, ws_send_self, ws_recv, z_send, z_recv, c_send, c_recv, h_send, h_recv, p_send, p_recv, s_send, s_recv,
):
    dp = lax.axis_index("dp")
    t = lax.axis_index("tensor")
    y_hi, z, core = dp // (2 * NZ), rem(dp // 2, NZ), rem(dp, 2)
    x, y_lo = t // 2, rem(t, 2)

    def dev(x, y_lo, y_hi, z, core):
        return ((y_hi * NZ + z) * 2 + core, x * 2 + y_lo)

    def flip(bit, by):
        return rem(bit + by, 2)

    def bring(i):
        src = (gain_in, wq_in, wk_in, wv_in, h_in, bq_in, bk_in, bv_in)[i]
        dst = (gain_ref, wq_ref, wk_ref, wv_ref, h_ref, bq_ref, bk_ref, bv_ref)[i]
        return pltpu.make_async_copy(src, dst, in_sem.at[i])

    for i in range(8):
        bring(i).start()

    barrier = pltpu.get_barrier_semaphore()
    peers = []
    for r in range(1, 32):
        peers.append(dev(rem(x + r % 4, 4), flip(y_lo, r // 4 % 2), flip(y_hi, r // 8 % 2), z, flip(core, r // 16)))
    up, down = rem(z + 1, NZ), rem(z + NZ - 1, NZ)
    up_dev, down_dev = dev(x, y_lo, y_hi, up, core), dev(x, y_lo, y_hi, down, core)
    peers += [up_dev, down_dev]
    for d in peers:
        pl.semaphore_signal(barrier, inc=1, device_id=d, device_id_type=MESH)

    for i in range(4):
        bring(i).wait()
    g = gain_ref[...].astype(F32)
    g_row = jnp.sum(jnp.where(lax.broadcasted_iota(jnp.int32, g.shape, 0) == dp, g, 0.0), axis=0, keepdims=True)
    lane = lax.broadcasted_iota(jnp.int32, (16, 128), 1)
    sub = lax.broadcasted_iota(jnp.int32, (16, 128), 0)
    g_col = jnp.sum(jnp.where(lane == sub + 16 * t, g_row, 0.0), axis=1, keepdims=True)
    for yh_d in range(2):
        for yl_d in range(2):
            for k in range(2):
                for e in range(2):
                    td = 4 * e + 2 * k + yl_d
                    first = (wk_ref if yh_d == 0 else wv_ref)[:, 128 * td : 128 * td + 128]
                    q0 = 512 * td + 256 * yh_d
                    parts = (first, wq_ref[:, q0 : q0 + 128], wq_ref[:, q0 + 128 : q0 + 256])
                    for j in range(3):
                        ws[j, (yh_d * 2 + yl_d) * 2 + k, :, 128 * e : 128 * e + 128] = (
                            parts[j].astype(F32) * g_col
                        ).astype(BF16)
    x0, x1 = rem(x, 2), x // 2

    pl.semaphore_wait(barrier, len(peers))

    def remote(src, dst, send, recv, device):
        pltpu.make_async_remote_copy(
            src_ref=src, dst_ref=dst, send_sem=send, recv_sem=recv, device_id=device, device_id_type=MESH
        ).start()

    def wait(ref, sem):
        pltpu.make_async_copy(ref, ref, sem).wait()

    slot_w = pl.ds(pl.multiple_of(16 * t, 16), 16)

    def shuffle(j):
        for r in range(8):
            yl_d, yh_d, k = flip(y_lo, r % 2), flip(y_hi, r // 2 % 2), flip(x0, r // 4)
            src = ws.at[j, (yh_d * 2 + yl_d) * 2 + k]
            dst = wb.at[j, core, slot_w, :]
            to = dev(2 * y_hi + k, yl_d, yh_d, z, core)
            if r > 0:
                remote(src, dst, ws_send, ws_recv.at[j], to)
            else:

                @pl.when(x1 == y_hi)
                def _():
                    pltpu.make_async_copy(src, dst, ws_recv.at[j]).start()

                @pl.when(x1 != y_hi)
                def _():
                    remote(src, dst, ws_send_self, ws_recv.at[j], to)

    for j in range(3):
        shuffle(j)

    for i in range(4, 8):
        bring(i).wait()
    piece = (y_hi * 4 + rem(t, 4)) * 8
    for u in range(8):
        a5[piece + u] = h_ref[:, 128 * u : 128 * u + 128]

    pair = dev(2 * x1 + 1 - x0, y_lo, y_hi, z, core)
    pair_piece = (y_hi * 4 + 2 * (1 - x0) + y_lo) * 8

    def row(r):
        return flip(y_lo, r % 2), flip(y_hi, r // 2)

    def move(base, lo, n, sem, to):
        at = a5.at[pl.ds(base + lo, n)]
        remote(at, at, h_send, h_recv.at[sem], to)

    def own_x(lo, n, sem):
        move(piece, lo, n, sem, pair)

    def own_y(r, lo, n, sem):
        yl, yh = row(r)
        move(piece, lo, n, sem, dev(x, yl, yh, z, core))

    def pair_y(r):
        yl, yh = row(r)
        move(pair_piece, 0, U, 5, dev(x, yl, yh, z, core))

    def got(n, sem):
        wait(a5.at[pl.ds(0, n)], h_recv.at[sem])

    def pass_x(r):
        got(8 - U, 1 + r)
        yl, yh = row(r)
        move((yh * 4 + 2 * x0 + yl) * 8, U, 8 - U, 7, pair)

    own_x(0, U, 0)
    for r in (1, 3):
        own_y(r, U, 8 - U, 1 + r)

    def hidden_0():
        own_x(U, 8 - U, 1)
        got(U, 0)
        pair_y(1)
        pair_y(3)

    def hidden_1():
        own_y(2, U, 8 - U, 3)
        pass_x(1)
        pass_x(3)

    def hidden_2():
        own_y(1, 0, U, 6)
        own_y(3, 0, U, 6)

    def hidden_4():
        own_y(2, 0, U, 6)
        pair_y(2)
        pass_x(2)

    def wait_hidden():
        got(8 - U, 1)
        got(3 * U, 5)
        got(3 * U, 6)
        got(3 * (8 - U), 7)

    me = core
    other = 1 - core

    def rows(p, half, lo=0, n=128):
        return pl.ds(p * 256 + half * 128 + lo, n)

    def z_copy(way, j, src_rows, dst_rows, sub_id, step):
        remote(
            wb.at[j, me, src_rows, :], wb.at[j, me, dst_rows, :], z_send, z_recv.at[way, sub_id, step - 1],
            up_dev if way == 0 else down_dev,
        )

    def to_core(j, at):
        remote(wb.at[j, me, at, :], wb.at[j, me, at, :], c_send, c_recv.at[j], dev(x, y_lo, y_hi, z, other))

    subs = []
    for j in range(3):
        n = 128 // SPLIT[j]
        subs += [(j, n * q, n) for q in range(SPLIT[j])]

    def own(cycle):
        for si, (j, lo_row, n) in enumerate(subs):
            if LATE[j] == cycle:
                if lo_row == 0:
                    wait(wb.at[j, me, rows(0, 0), :], ws_recv.at[j])
                for way in range(2):
                    z_copy(way, j, rows(0, 0, lo_row, n), rows(1, way, lo_row, n), si, 1)

    own(0)
    hidden_0()

    h = h_ref[...].astype(F32)
    sq = h * h
    hi = sq.astype(BF16)
    lo = (sq - hi.astype(F32)).astype(BF16)
    ones = jnp.ones((8, 1024), BF16)
    nt = (((1,), (1,)), ((), ()))
    ssb[0] = lax.dot_general(ones, hi, nt, preferred_element_type=F32) + lax.dot_general(
        ones, lo, nt, preferred_element_type=F32
    )
    for r in range(1, 8):
        remote(ssb.at[0], ssb.at[r], s_send, s_recv, dev(rem(x + r % 4, 4), flip(y_lo, r // 4), y_hi, z, core))

    def first_tables():
        ends, starts, total = [], [], 0
        for r in range(ROLLS):
            starts.append(total)
            total = total + len_ref[0, r]
            ends.append(total)
        tok = lax.broadcasted_iota(jnp.int32, (TOK, 128), 0)
        begin = jnp.zeros((TOK, 128), jnp.int32)
        for r in range(1, ROLLS):
            begin = jnp.where(tok >= ends[r - 1], starts[r], begin)
        d = lax.broadcasted_iota(jnp.int32, (TOK, 128), 1)
        half = rem(d, 64).astype(F32)
        freq = jnp.exp(half * (-2.0 / HD * math.log(BASE)))
        angle = (tok - begin).astype(F32) * freq
        cos_t[...] = jnp.cos(angle)
        s = jnp.sin(angle)
        sin_t[...] = jnp.where(d < 64, -s, s)
        for q in range(2):
            col = d + 128 * q
            mask_t[:, 128 * q : 128 * q + 128] = jnp.where((col >= begin) & (col <= tok), 0.0, NEG)

    def page_tables():
        ends, starts, total = [], [], 0
        for r in range(ROLLS):
            starts.append(total)
            total = total + len_ref[0, r]
        n = lax.broadcasted_iota(jnp.int32, (PAGES_REP * PAGE, 128), 0)
        page, slot = n // PAGE, rem(n, PAGE)
        src = jnp.full(n.shape, -1, jnp.int32)
        for e in range(PAGES_REP):
            r, b = e // BLOCKS, e % BLOCKS
            at = b * PAGE + slot
            src = jnp.where((page == pt_ref[0, e]) & (at < len_ref[0, r]), starts[r] + at, src)
        col = lax.broadcasted_iota(jnp.int32, (PAGES_REP * PAGE, 128), 1)
        for q in range(2):
            hot_t[:, 128 * q : 128 * q + 128] = jnp.where(src == col + 128 * q, 1.0, 0.0).astype(BF16)

    def relay(tk, k):
        for p in range(8):
            m1 = rem(z + NZ - p, NZ)
            m2 = rem(z + p, NZ) if p else rem(z + 8, NZ)
            a2[tk, k, :, 256 * p : 256 * p + 128] = a5[tk * 32 + 2 * m1 + k]
            a2[tk, k, :, 256 * p + 128 : 256 * p + 256] = a5[tk * 32 + 2 * m2 + k]

    def product(j, far):
        tk = 1 - y_hi if far else y_hi
        if far:
            wait(wb.at[j, other], c_recv.at[j])
        part = jnp.dot(a2[tk, 0], wb[j, 0], preferred_element_type=F32) + jnp.dot(
            a2[tk, 1], wb[j, 1], preferred_element_type=F32
        )
        part = part.astype(BF16)
        for e in range(2):
            ps[j, tk * 2 + e] = part[:, 128 * e : 128 * e + 128]
        for r in (3, 2) if far else (1,):
            e = flip(x1, r % 2)
            remote(
                ps.at[j, tk * 2 + e], rs.at[j, r], p_send, p_recv.at[j], dev(2 * e + x0, y_lo, tk, z, core)
            )

    P_ = functools.partial
    tasks = {
        1: [hidden_1], 2: [hidden_2, first_tables], 3: [page_tables], 4: [hidden_4],
        WH: [wait_hidden, P_(relay, 0, 0), P_(relay, 0, 1)], WH + 1: [P_(relay, 1, 0), P_(relay, 1, 1)],
    }
    last = max(LATE) + 8
    queue = []
    for cycle in range(1, last + 1):
        for si, (j, lo_row, n) in enumerate(subs):
            step = cycle - LATE[j]
            if not 1 <= step <= 8:
                continue
            half = n // 2
            for way in range(2):
                sem = z_recv.at[way, si, step - 1]
                lo2 = lo_row + way * half
                if step < 8:
                    at = rows(step, way, lo_row, n)
                    wait(wb.at[j, me, at, :], sem)
                    if step < 7:
                        z_copy(way, j, at, rows(step + 1, way, lo_row, n), si, step + 1)
                    else:
                        z_copy(way, j, rows(7, way, lo2, half), rows(0, 1, lo2, half), si, 8)
                else:
                    wait(wb.at[j, me, rows(0, 1, lo2, half), :], sem)
        own(cycle)
        for j in range(3):
            step = cycle - LATE[j]
            if step == 1:
                to_core(j, rows(0, 0))
            if 1 <= step < 8:
                for way in range(2):
                    to_core(j, rows(step, way))
            if step == 8:
                to_core(j, rows(0, 1))
                queue += [P_(product, j, True), P_(product, j, False)]
        if cycle in tasks:
            for f in tasks[cycle]:
                f()
        elif cycle < last:
            for _ in range(min(2, len(queue))):
                queue.pop(0)()
    for f in queue:
        f()

    wait(ssb.at[pl.ds(1, 7)], s_recv)
    total = ssb[0, 0:1, :]
    for r in range(1, 8):
        total = total + ssb[r, 0:1, :]
    scale_row = lax.rsqrt(total * (1.0 / D) + 1e-6)
    eye = lax.broadcasted_iota(jnp.int32, (TOK, TOK), 0) == lax.broadcasted_iota(jnp.int32, (TOK, TOK), 1)
    scale = jnp.sum(jnp.where(eye, scale_row, 0.0), axis=1, keepdims=True)

    def gathered(j):
        wait(rs.at[j, pl.ds(1, 3)], p_recv.at[j])
        own = ps[j, y_hi * 2 + x1].astype(F32) + rs[j, 1].astype(F32)
        far = rs[j, 2].astype(F32) + rs[j, 3].astype(F32)
        return (
            jnp.where(y_hi == 0, own, far) * scale,
            jnp.where(y_hi == 0, far, own) * scale,
        )

    def rope(v):
        return (v * cos_t[...] + pltpu.roll(v, 64, 1) * sin_t[...]).astype(BF16)

    key, value = gathered(0)
    key = rope(key + bk_ref[...].astype(F32))
    value = (value + bv_ref[...].astype(F32)).astype(BF16)
    kv_t[:, 0:128] = key
    kv_t[:, 128:256] = value
    page_ref[...] = jnp.dot(hot_t[...], kv_t[...], preferred_element_type=F32).astype(BF16)

    def attend(head, q):
        q = rope(q + bq_ref[head : head + 1].astype(F32))
        s = lax.dot_general(q, kv_t[:, 0:128], nt, preferred_element_type=F32) * HD ** (-0.5) + mask_t[...]
        w = jnp.exp(s - jnp.max(s, axis=-1, keepdims=True))
        w = (w / jnp.sum(w, axis=-1, keepdims=True)).astype(BF16)
        att_ref[:, 128 * head : 128 * head + 128] = jnp.dot(
            w, kv_t[:, 128:256], preferred_element_type=F32
        ).astype(BF16)

    for j in (1, 2):
        low, high = gathered(j)
        attend(j - 1, low)
        attend(j + 1, high)

    wait(ws.at[:, pl.ds(0, 7)], ws_send)

    @pl.when(x1 != y_hi)
    def _():
        wait(ws.at[:, 0], ws_send_self)

    wait(a5.at[pl.ds(0, 56)], h_send)
    wait(ssb.at[pl.ds(1, 7)], s_send)
    wait(wb.at[:, 0, pl.ds(0, 1920), :], z_send)
    wait(wb.at[:, 0], c_send)
    wait(rs.at[:, pl.ds(1, 3)], p_send)


def on_device(hidden, gain, wq, wk, wv, bq, bk, bv, lengths, table):
    hbm = pl.BlockSpec(memory_space=pltpu.MemorySpace.HBM)
    vmem = pl.BlockSpec(memory_space=pltpu.VMEM)
    smem = pl.BlockSpec(memory_space=pltpu.SMEM)
    dma = pltpu.SemaphoreType.DMA
    att, pages = pl.pallas_call(
        kernel,
        out_shape=(
            jax.ShapeDtypeStruct((TOK, 4 * HD), BF16),
            jax.ShapeDtypeStruct((PAGES_REP * PAGE, 2 * HD), BF16),
        ),
        in_specs=[hbm] * 8 + [smem] * 2,
        out_specs=(vmem, vmem),
        scratch_shapes=[
            *[
                pltpu.VMEM(s, BF16)
                for s in ((TOK, 1024), (64, 128), (16, 4096), (16, 1024), (16, 1024), (4, 128), (1, 128), (1, 128))
            ],
            dma((8,)),
            pltpu.VMEM((3, 8, 16, 256), BF16),
            pltpu.VMEM((3, 2, 2048, 256), BF16),
            pltpu.VMEM((64, TOK, 128), BF16),
            pltpu.VMEM((2, 2, TOK, 2048), BF16),
            pltpu.VMEM((3, 4, TOK, 128), BF16),
            pltpu.VMEM((3, 4, TOK, 128), BF16),
            pltpu.VMEM((8, 8, TOK), F32),
            pltpu.VMEM((TOK, 128), F32),
            pltpu.VMEM((TOK, 128), F32),
            pltpu.VMEM((TOK, TOK), F32),
            pltpu.VMEM((PAGES_REP * PAGE, TOK), BF16),
            pltpu.VMEM((TOK, 256), BF16),
            dma, dma, dma((3,)), dma, dma((2, 6, 8)), dma, dma((3,)), dma, dma((8,)), dma, dma((3,)), dma, dma,
        ],
        compiler_params=pltpu.CompilerParams(
            collective_id=0, has_side_effects=True, vmem_limit_bytes=60 * 2**20
        ),
        name="handover",
    )(
        hidden, gain.reshape(64, 128), wq, wk, wv, bq.reshape(4, -1), bk.reshape(1, -1), bv.reshape(1, -1),
        lengths, table,
    )
    return att, pages.reshape(PAGES_REP, PAGE, 2 * HD)


def solution(mesh):
    placed = (
        P("dp", "tensor"),
        P(),
        P(("dp", "tensor"), None),
        P(("dp", "tensor"), None),
        P(("dp", "tensor"), None),
        P("tensor"),
        P("tensor"),
        P("tensor"),
        P("dp", None),
        P("dp", None),
    )
    return jax.shard_map(
        on_device,
        mesh=mesh,
        in_specs=placed,
        out_specs=(P("dp", "tensor"), P("dp", None, "tensor")),
        check_vma=False,
    )
```

```python
import functools
import math

import jax
import jax.numpy as jnp
from jax import lax
from jax.experimental import pallas as pl
from jax.experimental.pallas import tpu as pltpu
from jax.sharding import PartitionSpec as P

MESH = pl.DeviceIdType.MESH
HD = 128
ROLLS = 4
PAGE = 32
BLOCKS = 4
PAGES_REP = 16
TOK = 256
D = 8192
NZ = 16
BASE = 1000000.0
F32 = jnp.float32
BF16 = jnp.bfloat16
NEG = -1e30
LATE = (0, 0, 1)
SPLIT = (2, 2, 2)
WH = 7
U = 3


def rem(a, n):
    return lax.rem(a, n)


def kernel(
    h_in, gain_in, wq_in, wk_in, wv_in, bq_in, bk_in, bv_in, len_ref, pt_ref,
    att_ref, page_ref,
    h_ref, gain_ref, wq_ref, wk_ref, wv_ref, bq_ref, bk_ref, bv_ref, in_sem,
    ws, wb, a5, a2, ps, rs, ssb, cos_t, sin_t, mask_t, hot_t, kv_t,
    ws_send, ws_send_self, ws_recv, z_send, z_recv, c_send, c_recv, h_send, h_recv, p_send, p_recv, s_send, s_recv,
):
    dp = lax.axis_index("dp")
    t = lax.axis_index("tensor")
    y_hi, z, core = dp // (2 * NZ), rem(dp // 2, NZ), rem(dp, 2)
    x, y_lo = t // 2, rem(t, 2)

    def dev(x, y_lo, y_hi, z, core):
        return ((y_hi * NZ + z) * 2 + core, x * 2 + y_lo)

    def flip(bit, by):
        return rem(bit + by, 2)

    def bring(i):
        src = (gain_in, wq_in, wk_in, wv_in, h_in, bq_in, bk_in, bv_in)[i]
        dst = (gain_ref, wq_ref, wk_ref, wv_ref, h_ref, bq_ref, bk_ref, bv_ref)[i]
        return pltpu.make_async_copy(src, dst, in_sem.at[i])

    for i in range(8):
        bring(i).start()

    barrier = pltpu.get_barrier_semaphore()
    peers = []
    for r in range(1, 32):
        peers.append(dev(rem(x + r % 4, 4), flip(y_lo, r // 4 % 2), flip(y_hi, r // 8 % 2), z, flip(core, r // 16)))
    up, down = rem(z + 1, NZ), rem(z + NZ - 1, NZ)
    up_dev, down_dev = dev(x, y_lo, y_hi, up, core), dev(x, y_lo, y_hi, down, core)
    peers += [up_dev, down_dev]
    for d in peers:
        pl.semaphore_signal(barrier, inc=1, device_id=d, device_id_type=MESH)

    for i in range(4):
        bring(i).wait()
    g = gain_ref[...].astype(F32)
    g_row = jnp.sum(jnp.where(lax.broadcasted_iota(jnp.int32, g.shape, 0) == dp, g, 0.0), axis=0, keepdims=True)
    lane = lax.broadcasted_iota(jnp.int32, (16, 128), 1)
    sub = lax.broadcasted_iota(jnp.int32, (16, 128), 0)
    g_col = jnp.sum(jnp.where(lane == sub + 16 * t, g_row, 0.0), axis=1, keepdims=True)
    for yh_d in range(2):
        for yl_d in range(2):
            for k in range(2):
                for e in range(2):
                    td = 4 * e + 2 * k + yl_d
                    first = (wk_ref if yh_d == 0 else wv_ref)[:, 128 * td : 128 * td + 128]
                    q0 = 512 * td + 256 * yh_d
                    parts = (first, wq_ref[:, q0 : q0 + 128], wq_ref[:, q0 + 128 : q0 + 256])
                    for j in range(3):
                        ws[j, (yh_d * 2 + yl_d) * 2 + k, :, 128 * e : 128 * e + 128] = (
                            parts[j].astype(F32) * g_col
                        ).astype(BF16)
    x0, x1 = rem(x, 2), x // 2

    pl.semaphore_wait(barrier, len(peers))

    def remote(src, dst, send, recv, device):
        pltpu.make_async_remote_copy(
            src_ref=src, dst_ref=dst, send_sem=send, recv_sem=recv, device_id=device, device_id_type=MESH
        ).start()

    def wait(ref, sem):
        pltpu.make_async_copy(ref, ref, sem).wait()

    slot_w = pl.ds(pl.multiple_of(16 * t, 16), 16)

    def shuffle(j):
        for r in range(8):
            yl_d, yh_d, k = flip(y_lo, r % 2), flip(y_hi, r // 2 % 2), flip(x0, r // 4)
            src = ws.at[j, (yh_d * 2 + yl_d) * 2 + k]
            dst = wb.at[j, core, slot_w, :]
            to = dev(2 * y_hi + k, yl_d, yh_d, z, core)
            if r > 0:
                remote(src, dst, ws_send, ws_recv.at[j], to)
            else:

                @pl.when(x1 == y_hi)
                def _():
                    pltpu.make_async_copy(src, dst, ws_recv.at[j]).start()

                @pl.when(x1 != y_hi)
                def _():
                    remote(src, dst, ws_send_self, ws_recv.at[j], to)

    for j in range(3):
        shuffle(j)

    for i in range(4, 8):
        bring(i).wait()
    piece = (y_hi * 4 + rem(t, 4)) * 8
    for u in range(8):
        a5[piece + u] = h_ref[:, 128 * u : 128 * u + 128]

    pair = dev(2 * x1 + 1 - x0, y_lo, y_hi, z, core)
    pair_piece = (y_hi * 4 + 2 * (1 - x0) + y_lo) * 8

    def row(r):
        return flip(y_lo, r % 2), flip(y_hi, r // 2)

    def move(base, lo, n, sem, to):
        at = a5.at[pl.ds(base + lo, n)]
        remote(at, at, h_send, h_recv.at[sem], to)

    def own_x(lo, n, sem):
        move(piece, lo, n, sem, pair)

    def own_y(r, lo, n, sem):
        yl, yh = row(r)
        move(piece, lo, n, sem, dev(x, yl, yh, z, core))

    def pair_y(r):
        yl, yh = row(r)
        move(pair_piece, 0, U, 5, dev(x, yl, yh, z, core))

    def got(n, sem):
        wait(a5.at[pl.ds(0, n)], h_recv.at[sem])

    def pass_x(r):
        got(8 - U, 1 + r)
        yl, yh = row(r)
        move((yh * 4 + 2 * x0 + yl) * 8, U, 8 - U, 7, pair)

    own_x(0, U, 0)
    for r in (1, 3):
        own_y(r, U, 8 - U, 1 + r)

    def hidden_0():
        own_x(U, 8 - U, 1)
        got(U, 0)
        pair_y(1)
        pair_y(3)

    def hidden_1():
        own_y(2, U, 8 - U, 3)
        pass_x(1)
        pass_x(3)

    def hidden_2():
        own_y(1, 0, U, 6)
        own_y(3, 0, U, 6)

    def hidden_4():
        own_y(2, 0, U, 6)
        pair_y(2)
        pass_x(2)

    def wait_hidden():
        got(8 - U, 1)
        got(3 * U, 5)
        got(3 * U, 6)
        got(3 * (8 - U), 7)

    me = core
    other = 1 - core

    def rows(p, half, lo=0, n=128):
        return pl.ds(p * 256 + half * 128 + lo, n)

    def z_copy(way, j, src_rows, dst_rows, sub_id, step):
        remote(
            wb.at[j, me, src_rows, :], wb.at[j, me, dst_rows, :], z_send, z_recv.at[way, sub_id, step - 1],
            up_dev if way == 0 else down_dev,
        )

    def to_core(j, at):
        remote(wb.at[j, me, at, :], wb.at[j, me, at, :], c_send, c_recv.at[j], dev(x, y_lo, y_hi, z, other))

    subs = []
    for j in range(3):
        n = 128 // SPLIT[j]
        subs += [(j, n * q, n) for q in range(SPLIT[j])]

    def own(cycle):
        for si, (j, lo_row, n) in enumerate(subs):
            if LATE[j] == cycle:
                if lo_row == 0:
                    wait(wb.at[j, me, rows(0, 0), :], ws_recv.at[j])
                for way in range(2):
                    z_copy(way, j, rows(0, 0, lo_row, n), rows(1, way, lo_row, n), si, 1)

    own(0)
    hidden_0()

    h = h_ref[...].astype(F32)
    sq = h * h
    hi = sq.astype(BF16)
    lo = (sq - hi.astype(F32)).astype(BF16)
    ones = jnp.ones((8, 1024), BF16)
    nt = (((1,), (1,)), ((), ()))
    ssb[0] = lax.dot_general(ones, hi, nt, preferred_element_type=F32) + lax.dot_general(
        ones, lo, nt, preferred_element_type=F32
    )
    for r in range(1, 8):
        remote(ssb.at[0], ssb.at[r], s_send, s_recv, dev(rem(x + r % 4, 4), flip(y_lo, r // 4), y_hi, z, core))

    def first_tables():
        ends, starts, total = [], [], 0
        for r in range(ROLLS):
            starts.append(total)
            total = total + len_ref[0, r]
            ends.append(total)
        tok = lax.broadcasted_iota(jnp.int32, (TOK, 128), 0)
        begin = jnp.zeros((TOK, 128), jnp.int32)
        for r in range(1, ROLLS):
            begin = jnp.where(tok >= ends[r - 1], starts[r], begin)
        d = lax.broadcasted_iota(jnp.int32, (TOK, 128), 1)
        half = rem(d, 64).astype(F32)
        freq = jnp.exp(half * (-2.0 / HD * math.log(BASE)))
        angle = (tok - begin).astype(F32) * freq
        cos_t[...] = jnp.cos(angle)
        s = jnp.sin(angle)
        sin_t[...] = jnp.where(d < 64, -s, s)
        for q in range(2):
            col = d + 128 * q
            mask_t[:, 128 * q : 128 * q + 128] = jnp.where((col >= begin) & (col <= tok), 0.0, NEG)

    def page_tables():
        ends, starts, total = [], [], 0
        for r in range(ROLLS):
            starts.append(total)
            total = total + len_ref[0, r]
        n = lax.broadcasted_iota(jnp.int32, (PAGES_REP * PAGE, 128), 0)
        page, slot = n // PAGE, rem(n, PAGE)
        src = jnp.full(n.shape, -1, jnp.int32)
        for e in range(PAGES_REP):
            r, b = e // BLOCKS, e % BLOCKS
            at = b * PAGE + slot
            src = jnp.where((page == pt_ref[0, e]) & (at < len_ref[0, r]), starts[r] + at, src)
        col = lax.broadcasted_iota(jnp.int32, (PAGES_REP * PAGE, 128), 1)
        for q in range(2):
            hot_t[:, 128 * q : 128 * q + 128] = jnp.where(src == col + 128 * q, 1.0, 0.0).astype(BF16)

    def relay(tk, k):
        for p in range(8):
            m1 = rem(z + NZ - p, NZ)
            m2 = rem(z + p, NZ) if p else rem(z + 8, NZ)
            a2[tk, k, :, 256 * p : 256 * p + 128] = a5[tk * 32 + 2 * m1 + k]
            a2[tk, k, :, 256 * p + 128 : 256 * p + 256] = a5[tk * 32 + 2 * m2 + k]

    def product(j, far):
        tk = 1 - y_hi if far else y_hi
        if far:
            wait(wb.at[j, other], c_recv.at[j])
        part = jnp.dot(a2[tk, 0], wb[j, 0], preferred_element_type=F32) + jnp.dot(
            a2[tk, 1], wb[j, 1], preferred_element_type=F32
        )
        part = part.astype(BF16)
        for e in range(2):
            ps[j, tk * 2 + e] = part[:, 128 * e : 128 * e + 128]
        for r in (3, 2) if far else (1,):
            e = flip(x1, r % 2)
            remote(
                ps.at[j, tk * 2 + e], rs.at[j, r], p_send, p_recv.at[j], dev(2 * e + x0, y_lo, tk, z, core)
            )

    P_ = functools.partial
    tasks = {
        1: [hidden_1], 2: [hidden_2, first_tables], 3: [page_tables], 4: [hidden_4],
        WH: [wait_hidden, P_(relay, 0, 0), P_(relay, 0, 1)], WH + 1: [P_(relay, 1, 0), P_(relay, 1, 1)],
    }
    last = max(LATE) + 8
    queue = []
    for cycle in range(1, last + 1):
        for si, (j, lo_row, n) in enumerate(subs):
            step = cycle - LATE[j]
            if not 1 <= step <= 8:
                continue
            half = n // 2
            for way in range(2):
                sem = z_recv.at[way, si, step - 1]
                lo2 = lo_row + way * half
                if step < 8:
                    at = rows(step, way, lo_row, n)
                    wait(wb.at[j, me, at, :], sem)
                    if step < 7:
                        z_copy(way, j, at, rows(step + 1, way, lo_row, n), si, step + 1)
                    else:
                        z_copy(way, j, rows(7, way, lo2, half), rows(0, 1, lo2, half), si, 8)
                else:
                    wait(wb.at[j, me, rows(0, 1, lo2, half), :], sem)
        own(cycle)
        for j in range(3):
            step = cycle - LATE[j]
            if step == 1:
                to_core(j, rows(0, 0))
            if 1 <= step < 8:
                for way in range(2):
                    to_core(j, rows(step, way))
            if step == 8:
                to_core(j, rows(0, 1))
                queue += [(j, True), (j, False)]
        for f in tasks.get(cycle, ()):
            f()
        if cycle == last - 1:
            for j, far in queue:
                product(j, far)
            queue = []
    for j, far in sorted(queue, key=lambda q: not q[1]):
        product(j, far)

    wait(ssb.at[pl.ds(1, 7)], s_recv)
    total = ssb[0, 0:1, :]
    for r in range(1, 8):
        total = total + ssb[r, 0:1, :]
    scale_row = lax.rsqrt(total * (1.0 / D) + 1e-6)
    eye = lax.broadcasted_iota(jnp.int32, (TOK, TOK), 0) == lax.broadcasted_iota(jnp.int32, (TOK, TOK), 1)
    scale = jnp.sum(jnp.where(eye, scale_row, 0.0), axis=1, keepdims=True)

    def gathered(j):
        wait(rs.at[j, pl.ds(1, 3)], p_recv.at[j])
        own = ps[j, y_hi * 2 + x1].astype(F32) + rs[j, 1].astype(F32)
        far = rs[j, 2].astype(F32) + rs[j, 3].astype(F32)
        return (
            jnp.where(y_hi == 0, own, far) * scale,
            jnp.where(y_hi == 0, far, own) * scale,
        )

    def rope(v):
        return (v * cos_t[...] + pltpu.roll(v, 64, 1) * sin_t[...]).astype(BF16)

    key, value = gathered(0)
    key = rope(key + bk_ref[...].astype(F32))
    value = (value + bv_ref[...].astype(F32)).astype(BF16)
    kv_t[:, 0:128] = key
    kv_t[:, 128:256] = value
    page_ref[...] = jnp.dot(hot_t[...], kv_t[...], preferred_element_type=F32).astype(BF16)

    def attend(head, q):
        q = rope(q + bq_ref[head : head + 1].astype(F32))
        s = lax.dot_general(q, kv_t[:, 0:128], nt, preferred_element_type=F32) * HD ** (-0.5) + mask_t[...]
        w = jnp.exp(s - jnp.max(s, axis=-1, keepdims=True))
        w = (w / jnp.sum(w, axis=-1, keepdims=True)).astype(BF16)
        att_ref[:, 128 * head : 128 * head + 128] = jnp.dot(
            w, kv_t[:, 128:256], preferred_element_type=F32
        ).astype(BF16)

    for j in (1, 2):
        low, high = gathered(j)
        attend(j - 1, low)
        attend(j + 1, high)

    wait(ws.at[:, pl.ds(0, 7)], ws_send)

    @pl.when(x1 != y_hi)
    def _():
        wait(ws.at[:, 0], ws_send_self)

    wait(a5.at[pl.ds(0, 56)], h_send)
    wait(ssb.at[pl.ds(1, 7)], s_send)
    wait(wb.at[:, 0, pl.ds(0, 1920), :], z_send)
    wait(wb.at[:, 0], c_send)
    wait(rs.at[:, pl.ds(1, 3)], p_send)


def on_device(hidden, gain, wq, wk, wv, bq, bk, bv, lengths, table):
    hbm = pl.BlockSpec(memory_space=pltpu.MemorySpace.HBM)
    vmem = pl.BlockSpec(memory_space=pltpu.VMEM)
    smem = pl.BlockSpec(memory_space=pltpu.SMEM)
    dma = pltpu.SemaphoreType.DMA
    att, pages = pl.pallas_call(
        kernel,
        out_shape=(
            jax.ShapeDtypeStruct((TOK, 4 * HD), BF16),
            jax.ShapeDtypeStruct((PAGES_REP * PAGE, 2 * HD), BF16),
        ),
        in_specs=[hbm] * 8 + [smem] * 2,
        out_specs=(vmem, vmem),
        scratch_shapes=[
            *[
                pltpu.VMEM(s, BF16)
                for s in ((TOK, 1024), (64, 128), (16, 4096), (16, 1024), (16, 1024), (4, 128), (1, 128), (1, 128))
            ],
            dma((8,)),
            pltpu.VMEM((3, 8, 16, 256), BF16),
            pltpu.VMEM((3, 2, 2048, 256), BF16),
            pltpu.VMEM((64, TOK, 128), BF16),
            pltpu.VMEM((2, 2, TOK, 2048), BF16),
            pltpu.VMEM((3, 4, TOK, 128), BF16),
            pltpu.VMEM((3, 4, TOK, 128), BF16),
            pltpu.VMEM((8, 8, TOK), F32),
            pltpu.VMEM((TOK, 128), F32),
            pltpu.VMEM((TOK, 128), F32),
            pltpu.VMEM((TOK, TOK), F32),
            pltpu.VMEM((PAGES_REP * PAGE, TOK), BF16),
            pltpu.VMEM((TOK, 256), BF16),
            dma, dma, dma((3,)), dma, dma((2, 6, 8)), dma, dma((3,)), dma, dma((8,)), dma, dma((3,)), dma, dma,
        ],
        compiler_params=pltpu.CompilerParams(
            collective_id=0, has_side_effects=True, vmem_limit_bytes=60 * 2**20
        ),
        name="handover",
    )(
        hidden, gain.reshape(64, 128), wq, wk, wv, bq.reshape(4, -1), bk.reshape(1, -1), bv.reshape(1, -1),
        lengths, table,
    )
    return att, pages.reshape(PAGES_REP, PAGE, 2 * HD)


def solution(mesh):
    placed = (
        P("dp", "tensor"),
        P(),
        P(("dp", "tensor"), None),
        P(("dp", "tensor"), None),
        P(("dp", "tensor"), None),
        P("tensor"),
        P("tensor"),
        P("tensor"),
        P("dp", None),
        P("dp", None),
    )
    return jax.shard_map(
        on_device,
        mesh=mesh,
        in_specs=placed,
        out_specs=(P("dp", "tensor"), P("dp", None, "tensor")),
        check_vma=False,
    )
```
